32 devices in a mesh: seq: 16 (over z, y, core), ch: 2 (over x).
Axes of the slice: x: 2, y: 2, z: 4, core: 2. Of those that a mesh axis runs over, the one named last changes fastest.
Arguments:
- inputs: bfloat16 [4, 4096, 1536], P(None, 'seq', 'ch'), may hold values from -6 to 6
- kernels: float32 [3, 3, 1536], P(None, None, 'ch'), may hold values from -3.5 to 3.5
- mixers: bfloat16 [3, 1536, 1536], P(None, None, 'ch'), may hold values from -0.15625 to 0.15625
- cotangent: bfloat16 [4, 4096, 1536], P(None, 'seq', 'ch'), may hold values from -6 to 6
Outputs:
- outputs: bfloat16 [4, 4096, 1536], P(None, 'seq', 'ch')
- input_grad: bfloat16 [4, 4096, 1536], P(None, 'seq', 'ch')
- mixer_grads: float32 [3, 1536, 1536], P(None, 'seq', 'ch')
The draws below stay inside these ranges and needn't reach their ends.
All inputs are finite; a program needn't handle non-finite values.
Results may differ from the reference program's by a relative error of at most 0.0075.
Values may be sent and summed in bfloat16 or wider, within the bound.
No kernel may reach another device: no remote copies, remote signals or barrier semaphores. Data moves between devices by JAX's collectives and lax.ppermute only.
A program may use at most 128 MiB of HBM per device.

```python
import math
import jax
import jax.numpy as jnp

C = 1536
SEQS = 4
BLOCKS = 3
BINS = 4096


def levels(key, dims, shards, low, high):
    factor_of, own = 1.0, jax.random.fold_in(key, 6)
    for axis_at, blocks in shards:
        steps = jnp.exp(jax.random.uniform(jax.random.fold_in(own, axis_at), (blocks,), jnp.float32, low / len(shards), high / len(shards)))
        factor_of = factor_of * jnp.repeat(steps, dims[axis_at] // blocks).reshape([-1 if axis == axis_at else 1 for axis in range(len(dims))])
    return factor_of


def gaussian(stream_key, dims, scale, limit, cuts=(), dtype=jnp.bfloat16):
    factor_of = levels(stream_key, dims, cuts, -0.22, 0.18) if cuts else 1.0
    values = jax.random.normal(stream_key, dims, jnp.float32) * scale * factor_of
    return jnp.minimum(jnp.maximum(values, -limit), limit).astype(dtype)


def setup_inputs(seed: int = 0) -> dict:
    splits = jax.random.split(jax.random.key(seed), 5)
    return {
        "inputs": gaussian(splits[0], (SEQS, BINS, C), 1.0, 6.0, ((1, 16), (2, 2))),
        "kernels": gaussian(splits[1], (BLOCKS, 3, C), 3 ** -0.5, 3.5, ((2, 2),), jnp.float32),
        "mixers": gaussian(splits[2], (BLOCKS, C, C), C ** -0.5, 0.15625, ((2, 2),)),
        "cotangent": gaussian(splits[3], (SEQS, BINS, C), 1.0, 6.0, ((1, 16), (2, 2))),
    }


dilations = (2, 4, 8)

def gelu_exact(value):
    return 0.5 * value * (1.0 + jax.scipy.special.erf(value * 0.7071067811865476))

def gelu_slope(value):
    return 0.5 * (1.0 + jax.scipy.special.erf(value * 0.7071067811865476)) + value * jnp.exp(-0.5 * value * value) * 0.3989422804014327

def reference(inputs, kernels, mixers, cotangent):
    seqs, bins, chans = inputs.shape
    current = inputs
    saved = []
    for block, width in enumerate(dilations):
        padded = jnp.pad(current.astype(jnp.float32), ((0, 0), (width, width), (0, 0)))
        pre = kernels[block, 0] * padded[:, 0:bins] + kernels[block, 1] * padded[:, width:width + bins] + kernels[block, 2] * padded[:, 2 * width:2 * width + bins]
        act = gelu_exact(pre).astype(jnp.bfloat16)
        mixed = jnp.dot(act.reshape(-1, chans), mixers[block], preferred_element_type=jnp.float32)
        current = (current.astype(jnp.float32) + mixed.reshape(seqs, bins, chans)).astype(jnp.bfloat16)
        saved.append((pre, act))
    scale = 1.0 / math.sqrt(seqs * bins)
    grad_list = [None, None, None]
    upper = cotangent
    for block in (2, 1, 0):
        width = dilations[block]
        pre, act = saved[block]
        flat = upper.reshape(-1, chans)
        back = jnp.dot(flat, mixers[block].T, preferred_element_type=jnp.float32).reshape(seqs, bins, chans)
        slope = (back * gelu_slope(pre)).astype(jnp.bfloat16)
        grad_list[block] = jnp.dot(act.reshape(-1, chans).T, flat, preferred_element_type=jnp.float32) * scale
        padded = jnp.pad(slope.astype(jnp.float32), ((0, 0), (width, width), (0, 0)))
        lower = upper.astype(jnp.float32) + kernels[block, 0] * padded[:, 2 * width:2 * width + bins] + kernels[block, 1] * padded[:, width:width + bins] + kernels[block, 2] * padded[:, 0:bins]
        upper = lower.astype(jnp.bfloat16)
    return (current, upper, jnp.stack(grad_list))
```

```python
import functools
import math

import jax
import jax.numpy as jnp
from jax import lax
from jax.experimental import pallas as pl
from jax.experimental.pallas import tpu as pltpu
from jax.sharding import PartitionSpec as P

DILATIONS = (2, 4, 8)
HX = 32
HE = 16
TILE = 256
BF16, F32 = jnp.bfloat16, jnp.float32
VMEM_BYTES = 58 * 1024 * 1024


def flip(value, axis, bit):
    count = lax.axis_size(axis)
    return lax.ppermute(value, axis, [(i, i ^ (1 << bit)) for i in range(count)])


def shift(value, step, other):
    n, m = lax.axis_size("seq"), lax.axis_size("ch")
    pairs = []
    for s in range(n):
        for c in range(m):
            if 0 <= s + step < n:
                target = (c ^ 1) if other else c
                pairs.append((s * m + c, (s + step) * m + target))
    return lax.ppermute(value, ("seq", "ch"), pairs)


def start_all(copies):
    for copy in copies:
        copy.start()


def wait_all(copies):
    for copy in copies:
        copy.wait()


def weight_copies(scal, mix, near, far, weights, sems, block, marks):
    c, part = scal[0], scal[1]
    half = mix.shape[1] // 2
    size = near.shape[1]
    per_half = half // size
    parts = 2 * near.shape[0]
    copies = []
    for h in range(2):
        copies.append(
            pltpu.make_async_copy(
                mix.at[block, pl.ds(pl.multiple_of((h ^ c) * half, half), half), :],
                weights.at[0, pl.ds(h * half, half), :],
                sems.at[h],
            )
        )
    for rel in range(parts):
        source = near if rel < parts // 2 else far
        place = part ^ marks[rel]
        row = ((place // per_half) ^ c) * half + (place % per_half) * size
        copies.append(
            pltpu.make_async_copy(
                source.at[rel % (parts // 2)],
                weights.at[1, pl.ds(pl.multiple_of(row, size), size), :],
                sems.at[2 + rel],
            )
        )
    return copies


def gather_copies(scal, own, partner, halos, buffer, sems, halo, skip):
    c = scal[0]
    lo_own, lo_other, hi_own, hi_other = halos
    seqs, bins, half = partner.shape
    pieces = []
    for q in range(seqs):
        for side, (main, lo, hi) in enumerate(((own, lo_own, hi_own), (partner, lo_other, hi_other))):
            cols = pl.ds(side * half, half)
            at = c * seqs + q if side == 0 else q
            pieces.append((main.at[at], buffer.at[q, pl.ds(halo, bins), cols]))
            pieces.append((lo.at[q, pl.ds(skip, halo), :], buffer.at[q, pl.ds(0, halo), cols]))
            pieces.append((hi.at[q, pl.ds(skip, halo), :], buffer.at[q, pl.ds(halo + bins, halo), cols]))
    return [pltpu.make_async_copy(a, b, sems.at[i]) for i, (a, b) in enumerate(pieces)]


def taps_of(taps, tile, half):
    side, at = divmod(tile * TILE, half)
    return [taps[side, k : k + 1, at : at + TILE] for k in range(3)]


def forward_kernel(block, first, last, marks, scal, *refs):
    if first:
        own, partner, l0, l1, h0, h1, taps, mix, near, far, nxt, act_out, slope_out, buffer, acts, weights, sems, wsems = refs
        loads = gather_copies(scal, own, partner, (l0, l1, h0, h1), buffer, sems, HX, 0)
        current = buffer
    else:
        current, taps, mix, near, far = refs[:5]
        if last:
            nxt, nxt_other, act_out, slope_out, acts, weights, wsems = refs[5:]
        else:
            nxt, act_out, slope_out, acts, weights, wsems = refs[5:]
        loads = []
    brings = weight_copies(scal, mix, near, far, weights, wsems, block, marks)
    start_all(loads)
    start_all(brings)
    wait_all(loads)
    seqs, rows, chans = current.shape
    half = chans // 2
    width = DILATIONS[block]
    bins = rows - 2 * HX
    edge = 0 if not last else HX - HE
    for q in range(seqs):
        for tile in range(chans // TILE):
            cols = slice(tile * TILE, (tile + 1) * TILE)
            k0, k1, k2 = taps_of(taps, tile, half)
            wide = current[q, :, cols].astype(F32)
            pre = k0 * pltpu.roll(wide, width, 0) + k1 * wide + k2 * pltpu.roll(wide, rows - width, 0)
            pre = pre[HX - HE : rows - (HX - HE)] if last else pre
            cdf = 0.5 * (1.0 + lax.erf(pre * 0.7071067811865476))
            slope = cdf + pre * jnp.exp(-0.5 * pre * pre) * 0.3989422804014327
            act = (pre * cdf).astype(BF16)
            if last:
                slope_out[q, :, cols] = slope.astype(BF16)
                acts[q, :, cols] = act[HE : HE + bins]
                act_out[q, :, cols] = act[HE : HE + bins]
            else:
                slope_out[q, :, cols] = slope[HX - HE : rows - (HX - HE)].astype(BF16)
                acts[q, :, cols] = act
                act_out[q, :, cols] = act[HX : HX + bins]
    wait_all(brings)
    for tile in range(chans // TILE):
        cols = slice(tile * TILE, (tile + 1) * TILE)
        side, at = divmod(tile * TILE, half)
        for q in range(seqs):
            mixed = jnp.dot(acts[q], weights[side, :, at : at + TILE], preferred_element_type=F32)
            if last:
                out = (current[q, HX : HX + bins, cols].astype(F32) + mixed).astype(BF16)
                (nxt, nxt_other)[side][q, :, at : at + TILE] = out
            else:
                nxt[q, :, cols] = (current[q, :, cols].astype(F32) + mixed).astype(BF16)
    if not last:

        @pl.when(scal[2] == 0)
        def _():
            nxt[:, 0:HX, :] = jnp.zeros((seqs, HX, chans), BF16)

        @pl.when(scal[3] == 0)
        def _():
            nxt[:, rows - HX : rows, :] = jnp.zeros((seqs, HX, chans), BF16)


def backward_kernel(block, first, last, marks, scale, scal, *refs):
    if first:
        own, partner, l0, l1, h0, h1 = refs[:6]
        refs = refs[6:]
    else:
        upper = refs[0]
        refs = refs[1:]
    act, slopes, taps, mix, near, far = refs[:6]
    refs = refs[6:]
    if last:
        lower, lower_other, keep, send = refs[:4]
        refs = refs[4:]
    else:
        lower, keep, send = refs[:3]
        refs = refs[3:]
    turned, weights, wsems = refs[:3]
    brings = weight_copies(scal, mix, near, far, weights, wsems, block, marks)
    loads = []
    if first:
        buffer, sems = refs[3:]
        loads = gather_copies(scal, own, partner, (l0, l1, h0, h1), buffer, sems, HE, HX)
        upper = buffer
    start_all(loads)
    start_all(brings)
    seqs, rows, chans = upper.shape
    half = chans // 2
    width = DILATIONS[block]
    bins = rows - 2 * HE
    c, s = scal[0], scal[4]
    count, size, _ = turned.shape
    for h in range(2):
        for q in range(seqs):
            flat = act[q, :, h * half : (h + 1) * half].T.astype(turned.dtype)
            for i in range(count // 2):
                rel = ((h ^ c) * (count // 2) + i) ^ s
                place = (rel & 1) * (count // 2) + (rel >> 1)
                turned[place, :, q * bins : (q + 1) * bins] = flat[i * size : (i + 1) * size]
    wait_all(loads)
    wait_all(brings)
    for q in range(seqs):
        for tile in range(chans // TILE):
            cols = slice(tile * TILE, (tile + 1) * TILE)
            side, at = divmod(tile * TILE, half)
            back = jnp.zeros((rows, TILE), F32)
            for g in range(2):
                back = back + lax.dot_general(
                    upper[q, :, g * half : (g + 1) * half],
                    weights[g, cols, :],
                    (((1,), (1,)), ((), ())),
                    preferred_element_type=F32,
                )
            slope = (back * slopes[q, :, cols].astype(F32)).astype(BF16).astype(F32)
            k0, k1, k2 = taps_of(taps, tile, half)
            new = upper[q, :, cols].astype(F32) + k0 * pltpu.roll(slope, rows - width, 0) + k1 * slope + k2 * pltpu.roll(slope, width, 0)
            new = new.astype(BF16)
            if last:
                (lower, lower_other)[side][q, :, at : at + TILE] = new[HE : HE + bins]
            else:
                lower[q, :, cols] = new
    if not last:

        @pl.when(scal[2] == 0)
        def _():
            lower[:, 0:HE, :] = jnp.zeros((seqs, HE, chans), BF16)

        @pl.when(scal[3] == 0)
        def _():
            lower[:, rows - HE : rows, :] = jnp.zeros((seqs, HE, chans), BF16)

    for part, target in enumerate((send, keep)):
        first_row = (1 - part) * (count // 2)
        left = turned[first_row : first_row + count // 2].reshape(count // 2 * size, seqs * bins).astype(BF16)
        for tile in range(chans // TILE):
            cols = slice(tile * TILE, (tile + 1) * TILE)
            side, at = divmod(tile * TILE, half)
            total = jnp.zeros((count // 2 * size, TILE), F32)
            for q in range(seqs):
                total = total + jnp.dot(
                    left[:, q * bins : (q + 1) * bins],
                    upper[q, HE : HE + bins, cols],
                    preferred_element_type=F32,
                )
            total = (total * scale).reshape(count // 2, size, TILE)
            target[side, :, :, at : at + TILE] = total.astype(BF16)


ANY = pl.BlockSpec(memory_space=pl.ANY)
VMEM = pl.BlockSpec(memory_space=pltpu.VMEM)
SMEM = pl.BlockSpec(memory_space=pltpu.SMEM)


def call(kernel, in_specs, outs, scratch, flops, bytes_accessed):
    return pl.pallas_call(
        kernel,
        in_specs=[SMEM] + in_specs,
        out_specs=[VMEM] * len(outs),
        out_shape=outs,
        scratch_shapes=scratch,
        compiler_params=pltpu.CompilerParams(vmem_limit_bytes=VMEM_BYTES),
        cost_estimate=pl.CostEstimate(flops=flops, bytes_accessed=bytes_accessed, transcendentals=0),
    )


def on_device(inputs, kernels, mixers, cotangent):
    all_seqs, bins, half = inputs.shape
    n, m = lax.axis_size("seq"), lax.axis_size("ch")
    s, c = lax.axis_index("seq"), lax.axis_index("ch")
    seqs, chans = all_seqs // m, half * m
    bits = n.bit_length() - 1
    blocks = mixers.shape[0]
    share_bits = min(3, bits)
    parts = 1 << share_bits
    piece = chans // parts
    part = s & (parts - 1)
    scal = jnp.stack([c, part, (s > 0).astype(jnp.int32), (s < n - 1).astype(jnp.int32), s]).astype(jnp.int32)

    def seqs_of(array, whose):
        return lax.dynamic_slice_in_dim(array, whose * seqs, seqs, 0)

    ups = jnp.concatenate([inputs[:, bins - HX :], cotangent[:, bins - HE :]], axis=1)
    downs = jnp.concatenate([inputs[:, :HX], cotangent[:, :HE]], axis=1)
    inputs_other = flip(seqs_of(inputs, 1 - c), "ch", 0)
    halos = (
        shift(seqs_of(ups, c), 1, False),
        shift(seqs_of(ups, 1 - c), 1, True),
        shift(seqs_of(downs, c), -1, False),
        shift(seqs_of(downs, 1 - c), -1, True),
    )
    taps_other = flip(kernels, "ch", 0)
    taps = [jnp.stack([kernels[b], taps_other[b]]) for b in range(blocks)]

    near, far, marks = [], [], []
    for b in range(blocks):
        held = flip(lax.dynamic_slice_in_dim(mixers[b], part * piece, piece, 0), "ch", 0)[None]
        own_marks = [0]
        order = range(1, share_bits) if b % 2 else range(share_bits - 1, 0, -1)
        for bit in order:
            held = jnp.concatenate([held, flip(held, "seq", bit)])
            own_marks = own_marks + [mark ^ (1 << bit) for mark in own_marks]
        near.append(held)
        far.append(flip(held, "seq", 0))
        marks.append(tuple(own_marks + [mark ^ 1 for mark in own_marks]))
    cot_other = flip(seqs_of(cotangent, 1 - c), "ch", 0)

    sd = jax.ShapeDtypeStruct
    rows_x, rows_e = bins + 2 * HX, bins + 2 * HE
    weight_scratch = [pltpu.VMEM((2, chans, half), BF16), pltpu.SemaphoreType.DMA((2 + parts,))]
    current = None
    saved = []
    for b in range(blocks):
        first, last = b == 0, b == blocks - 1
        outs = [sd((seqs, bins, half), BF16)] * 2 if last else [sd((seqs, rows_x, chans), BF16)]
        outs = outs + [sd((seqs, bins, chans), BF16), sd((seqs, rows_e, chans), BF16)]
        act_rows = bins if last else rows_x
        scratch = [pltpu.VMEM((seqs, act_rows, chans), BF16)] + weight_scratch
        if first:
            lead, specs = [inputs, inputs_other, *halos], [ANY] * 6
            scratch = [pltpu.VMEM((seqs, rows_x, chans), BF16), *scratch[:2], pltpu.SemaphoreType.DMA((6 * seqs,)), scratch[2]]
        else:
            lead, specs = [current], [VMEM]
        got = call(
            functools.partial(forward_kernel, b, first, last, marks[b]),
            specs + [VMEM, ANY, ANY, ANY],
            outs,
            scratch,
            2 * seqs * act_rows * chans * chans,
            12 * 1024 * 1024,
        )(scal, *lead, taps[b], mixers, near[b], far[b])
        if last:
            out_own, out_other, act, slope = got
        else:
            current, act, slope = got
        saved.append((act, slope))

    def both(own, sent):
        received = flip(sent, "ch", 0)
        return jnp.where(c == 0, jnp.concatenate([own, received]), jnp.concatenate([received, own]))

    outputs = both(out_own, out_other)

    scale = 1.0 / math.sqrt(all_seqs * bins * n)
    count = n
    size = chans // n
    turned_type = BF16 if size % 16 == 0 else F32
    grads = [None] * blocks
    upper = None
    for b in reversed(range(blocks)):
        first, last = b == blocks - 1, b == 0
        outs = [sd((seqs, bins, half), BF16)] * 2 if last else [sd((seqs, rows_e, chans), BF16)]
        outs = outs + [sd((2, count // 2, size, half), BF16)] * 2
        scratch = [pltpu.VMEM((count, size, seqs * bins), turned_type)] + weight_scratch
        if first:
            lead, specs = [cotangent, cot_other, *halos], [ANY] * 6
            scratch = scratch + [pltpu.VMEM((seqs, rows_e, chans), BF16), pltpu.SemaphoreType.DMA((6 * seqs,))]
        else:
            lead, specs = [upper], [VMEM]
        got = call(
            functools.partial(backward_kernel, b, first, last, marks[b], scale),
            specs + [VMEM, VMEM, VMEM, ANY, ANY, ANY],
            outs,
            scratch,
            2 * seqs * (rows_e + bins) * chans * chans,
            20 * 1024 * 1024,
        )(scal, *lead, *saved[b], taps[b], mixers, near[b], far[b])
        if last:
            in_own, in_other, keep, send = got
        else:
            upper, keep, send = got
        total = keep.astype(F32) + flip(send, "seq", 0).astype(F32)
        total = total.reshape((2,) * bits + (size, half))
        dims = ["ch"] + list(range(bits - 1, 0, -1))
        if bits == 4:
            order = {2: [2, 3, 1, "ch"], 1: [1, 2, 3, "ch"], 0: [1, "ch", 2, 3]}[b % 3]
        else:
            order = list(range(1, bits)) + ["ch"]
        for step in order:
            at = dims.index(step)
            dims.pop(at)
            kept = lax.index_in_dim(total, 0, at, keepdims=False)
            sent = lax.index_in_dim(total, 1, at, keepdims=False).astype(BF16)
            got_back = flip(sent, "ch", 0) if step == "ch" else flip(sent, "seq", step)
            total = kept + got_back.astype(F32)
        grads[b] = total
    input_grad = both(in_own, in_other)
    return outputs, input_grad, jnp.stack(grads)


def solution(mesh):
    placed = (P(None, "seq", "ch"), P(None, None, "ch"), P(None, None, "ch"), P(None, "seq", "ch"))
    return jax.shard_map(
        on_device,
        mesh=mesh,
        in_specs=placed,
        out_specs=(P(None, "seq", "ch"), P(None, "seq", "ch"), P(None, "seq", "ch")),
        check_vma=False,
    )
```

```python
import functools
import math

import jax
import jax.numpy as jnp
from jax import lax
from jax.experimental import pallas as pl
from jax.experimental.pallas import tpu as pltpu
from jax.sharding import PartitionSpec as P

DILATIONS = (2, 4, 8)
HX = 32
HE = 16
TILE = 256
BF16, F32 = jnp.bfloat16, jnp.float32
VMEM_BYTES = 28 * 1024 * 1024


def flip(value, axis, bit):
    count = lax.axis_size(axis)
    return lax.ppermute(value, axis, [(i, i ^ (1 << bit)) for i in range(count)])


def shift(value, step):
    count = lax.axis_size("seq")
    return lax.ppermute(value, "seq", [(i, i + step) for i in range(count) if 0 <= i + step < count])


def start_all(copies):
    for copy in copies:
        copy.start()


def wait_all(copies):
    for copy in copies:
        copy.wait()


def weight_copies(mix, near, far, weights, sems, block, marks):
    c = lax.axis_index("ch")
    half = mix.shape[1] // 2
    size = near.shape[1]
    per_half = half // size
    parts = 2 * near.shape[0]
    part = lax.axis_index("seq") % parts
    copies = []
    for h in range(2):
        copies.append(
            pltpu.make_async_copy(
                mix.at[block, pl.ds(pl.multiple_of((h ^ c) * half, half), half), :],
                weights.at[0, pl.ds(h * half, half), :],
                sems.at[h],
            )
        )
    for rel in range(parts):
        source = near if rel < parts // 2 else far
        place = part ^ marks[rel]
        row = ((place // per_half) ^ c) * half + (place % per_half) * size
        copies.append(
            pltpu.make_async_copy(
                source.at[rel % (parts // 2)],
                weights.at[1, pl.ds(pl.multiple_of(row, size), size), :],
                sems.at[2 + rel],
            )
        )
    return copies


def gather_copies(own, lo_own, hi_own, partner, buffer, sems, halo, skip):
    c = lax.axis_index("ch")
    seqs = buffer.shape[0]
    bins, half = own.shape[1:]
    low, main, high = pl.ds(0, halo), pl.ds(halo, bins), pl.ds(halo + bins, halo)
    cols = [pl.ds(side * half, half) for side in range(2)]
    pieces = []
    for q in range(seqs):
        at = c * seqs + q
        pieces.append((own.at[at], buffer.at[q, main, cols[0]]))
        pieces.append((lo_own.at[at, pl.ds(skip, halo), :], buffer.at[q, low, cols[0]]))
        pieces.append((hi_own.at[at, pl.ds(skip, halo), :], buffer.at[q, high, cols[0]]))
        other, row = (partner, q) if not isinstance(partner, (list, tuple)) else (partner[q], 0)
        pieces.append((other.at[row, pl.ds(0, bins), :], buffer.at[q, main, cols[1]]))
        pieces.append((other.at[row, pl.ds(bins, halo), :], buffer.at[q, low, cols[1]]))
        pieces.append((other.at[row, pl.ds(bins + halo, halo), :], buffer.at[q, high, cols[1]]))
    return [pltpu.make_async_copy(a, b, sems.at[i]) for i, (a, b) in enumerate(pieces)]


def taps_of(taps, block, tile):
    side, at = divmod(tile * TILE, taps[0].shape[2])
    return [taps[side][block, k : k + 1, at : at + TILE] for k in range(3)]


def activations(block, taps, current, q, tile, keep_rows):
    rows = current.shape[1]
    width = DILATIONS[block]
    cols = slice(tile * TILE, (tile + 1) * TILE)
    k0, k1, k2 = taps_of(taps, block, tile)
    wide = current[q, :, cols].astype(F32)
    pre = k0 * pltpu.roll(wide, width, 0) + k1 * wide + k2 * pltpu.roll(wide, rows - width, 0)
    pre = pre[keep_rows]
    cdf = 0.5 * (1.0 + lax.erf(pre * 0.7071067811865476))
    slope = cdf + pre * jnp.exp(-0.5 * pre * pre) * 0.3989422804014327
    return (pre * cdf).astype(BF16), slope.astype(BF16)


def zero_outside(array, halo):
    seqs, rows, chans = array.shape
    at = lax.axis_index("seq")

    @pl.when(at == 0)
    def _():
        array[:, 0:halo, :] = jnp.zeros((seqs, halo, chans), BF16)

    @pl.when(at == lax.axis_size("seq") - 1)
    def _():
        array[:, rows - halo : rows, :] = jnp.zeros((seqs, halo, chans), BF16)


def mix_tile(acts, weights, tile):
    half = weights.shape[2]
    side, at = divmod(tile * TILE, half)
    return jnp.dot(acts, weights[side, :, at : at + TILE], preferred_element_type=F32)


def forward_kernel(block, first, marks, *refs):
    if first:
        own, lo, hi, partner, t0, t1, mix, near, far, nxt, act_out, slope_out, acts, weights, wsems, current, sems = refs
        loads = gather_copies(own, lo, hi, partner, current, sems, HX, 0)
    else:
        current, t0, t1, mix, near, far, nxt, act_out, slope_out, acts, weights, wsems = refs
        loads = []
    brings = weight_copies(mix, near, far, weights, wsems, block, marks)
    start_all(loads)
    start_all(brings)
    wait_all(loads)
    seqs, rows, chans = current.shape
    bins = rows - 2 * HX
    edge = HX - HE
    for q in range(seqs):
        for tile in range(chans // TILE):
            cols = slice(tile * TILE, (tile + 1) * TILE)
            act, slope = activations(block, (t0, t1), current, q, tile, slice(None))
            slope_out[q, :, cols] = slope[edge : rows - edge]
            acts[q, :, cols] = act
            act_out[q, :, cols] = act[HX : HX + bins]
    wait_all(brings)
    for tile in range(chans // TILE):
        cols = slice(tile * TILE, (tile + 1) * TILE)
        for q in range(seqs):
            nxt[q, :, cols] = (current[q, :, cols].astype(F32) + mix_tile(acts[q], weights, tile)).astype(BF16)
    zero_outside(nxt, HX)


def gradient(act, upper, turned, keep, send, scale):
    seqs, bins, chans = act.shape
    half = chans // 2
    c, s = lax.axis_index("ch"), lax.axis_index("seq")
    count, size, _ = turned.shape
    for h in range(2):
        for q in range(seqs):
            flat = act[q, :, h * half : (h + 1) * half].T.astype(turned.dtype)
            for i in range(count // 2):
                rel = ((h ^ c) * (count // 2) + i) ^ s
                place = (rel & 1) * (count // 2) + (rel >> 1)
                turned[place, :, q * bins : (q + 1) * bins] = flat[i * size : (i + 1) * size]
    for part, target in enumerate((keep, send)):
        first_row = part * (count // 2)
        left = turned[first_row : first_row + count // 2].reshape(count // 2 * size, seqs * bins).astype(BF16)
        for tile in range(chans // TILE):
            cols = slice(tile * TILE, (tile + 1) * TILE)
            side, at = divmod(tile * TILE, half)
            total = sum(
                jnp.dot(left[:, q * bins : (q + 1) * bins], upper[q, HE : HE + bins, cols], preferred_element_type=F32)
                for q in range(seqs)
            )
            total = (total * scale).reshape(count // 2, size, TILE)
            target[side, :, :, at : at + TILE] = total.astype(BF16)


def turn_kernel(block, scale, *refs):
    current, own, lo, hi, p0, p1, t0, t1, act, slope_out, upper, keep, send, turned, sems = refs
    loads = gather_copies(own, lo, hi, (p0, p1), upper, sems, HE, HX)
    start_all(loads)
    seqs, rows, chans = current.shape
    edge = HX - HE
    for q in range(seqs):
        for tile in range(chans // TILE):
            cols = slice(tile * TILE, (tile + 1) * TILE)
            value, slope = activations(block, (t0, t1), current, q, tile, slice(edge, rows - edge))
            slope_out[q, :, cols] = slope
            act[q, :, cols] = value[HE : HE + act.shape[1]]
    wait_all(loads)
    gradient(act, upper, turned, keep, send, scale)


def gradient_kernel(scale, act, upper, keep, send, turned):
    gradient(act, upper, turned, keep, send, scale)


def backward_kernel(block, top, last, marks, scale, *refs):
    if top:
        current, act, upper, slopes, t0, t1, mix, near, far, out, *out_others, lower, weights, wsems = refs
    elif last:
        upper, slopes, t0, t1, mix, near, far, lower, lower_other, weights, wsems = refs
    else:
        upper, slopes, act, t0, t1, mix, near, far, lower, keep, send, weights, wsems, turned = refs
    brings = weight_copies(mix, near, far, weights, wsems, block, marks)
    start_all(brings)
    if not top and not last:
        gradient(act, upper, turned, keep, send, scale)
    wait_all(brings)
    seqs, rows, chans = upper.shape
    half = chans // 2
    width = DILATIONS[block]
    bins = rows - 2 * HE
    if top:
        for tile in range(chans // TILE):
            cols = slice(tile * TILE, (tile + 1) * TILE)
            side, at = divmod(tile * TILE, half)
            for q in range(seqs):
                mixed = mix_tile(act[q], weights, tile)
                value = (current[q, HX : HX + bins, cols].astype(F32) + mixed).astype(BF16)
                if side:
                    out_others[q][0, :, at : at + TILE] = value
                else:
                    out[q, :, at : at + TILE] = value
    for q in range(seqs):
        for tile in range(chans // TILE):
            cols = slice(tile * TILE, (tile + 1) * TILE)
            side, at = divmod(tile * TILE, half)
            back = sum(
                lax.dot_general(
                    upper[q, :, g * half : (g + 1) * half],
                    weights[g, cols, :],
                    (((1,), (1,)), ((), ())),
                    preferred_element_type=F32,
                )
                for g in range(2)
            )
            slope = (back * slopes[q, :, cols].astype(F32)).astype(BF16).astype(F32)
            k0, k1, k2 = taps_of((t0, t1), block, tile)
            new = upper[q, :, cols].astype(F32) + k0 * pltpu.roll(slope, rows - width, 0) + k1 * slope + k2 * pltpu.roll(slope, width, 0)
            new = new.astype(BF16)
            if last:
                (lower, lower_other)[side][q, :, at : at + TILE] = new[HE : HE + bins]
            else:
                lower[q, :, cols] = new
    if not last:
        zero_outside(lower, HE)


ANY = pl.BlockSpec(memory_space=pl.ANY)
VMEM = pl.BlockSpec(memory_space=pltpu.VMEM)


def call(kernel, in_specs, outs, scratch, micros, out_specs=None):
    return pl.pallas_call(
        kernel,
        in_specs=in_specs,
        out_specs=out_specs or [VMEM] * len(outs),
        out_shape=outs,
        scratch_shapes=scratch,
        compiler_params=pltpu.CompilerParams(vmem_limit_bytes=VMEM_BYTES),
        cost_estimate=pl.CostEstimate(flops=int(micros * 1.15e9), bytes_accessed=int(micros * 3.6e6), transcendentals=0),
    )


def pack_kernel(plan, operands, *refs):
    ins, outs, sems = refs[:operands], refs[operands:-1], refs[-1]
    copies = [
        pltpu.make_async_copy(ins[i].at[src], outs[o].at[dst], sems.at[k])
        for k, (i, src, o, dst) in enumerate(plan())
    ]
    start_all(copies)
    wait_all(copies)


def in_hbm(value):
    return pltpu.with_memory_space_constraint(value, pltpu.HBM)


def pack(plan, count, operands, outs):
    return call(
        functools.partial(pack_kernel, plan, len(operands)),
        [ANY] * len(operands),
        outs,
        [pltpu.SemaphoreType.DMA((count,))],
        1,
    )(*operands)


def fence_kernel(token, *refs):
    refs[-1][...] = token[...]


def fence(token, *others):
    return call(
        fence_kernel,
        [VMEM] + [ANY] * len(others),
        [jax.ShapeDtypeStruct(token.shape, token.dtype)],
        [],
        1,
    )(token, *others)[0]


def join(*values):
    return lax.optimization_barrier(values)


def on_device(inputs, kernels, mixers, cotangent):
    all_seqs, bins, half = inputs.shape
    n, m = lax.axis_size("seq"), lax.axis_size("ch")
    seqs, chans = all_seqs // m, half * m
    bits = n.bit_length() - 1
    blocks = mixers.shape[0]
    share_bits = min(3, bits)
    parts = 1 << share_bits
    piece = chans // parts
    sd = jax.ShapeDtypeStruct

    def ours(first, rows):
        return (pl.ds(lax.axis_index("ch") * seqs + first, seqs - first), rows)

    def theirs(first, rows, many=seqs):
        return (pl.ds((1 - lax.axis_index("ch")) * seqs + first, many), rows)

    everything = pl.ds(0, bins)
    inputs, cotangent, mixers = in_hbm(inputs), in_hbm(cotangent), in_hbm(mixers)

    def first_plan():
        plan = []
        for b in range(blocks):
            piece_rows = pl.ds(pl.multiple_of(lax.axis_index("seq") % parts * piece, piece), piece)
            plan.append((2, (b, piece_rows), 0, b))
        for place, (rows_x, rows_e) in enumerate(((pl.ds(bins - HX, HX), pl.ds(bins - HE, HE)), (pl.ds(0, HX), pl.ds(0, HE)))):
            plan.append((0, (slice(None), rows_x), 1 + place, (slice(None), pl.ds(0, HX))))
            plan.append((1, (slice(None), rows_e), 1 + place, (slice(None), pl.ds(HX, HE))))
        return plan

    seqs_shape = sd((seqs, bins, half), BF16)
    halo_shape = sd((all_seqs, HX + HE, half), BF16)
    sent, ups, downs = pack(first_plan, blocks + 4, [inputs, cotangent, mixers], [sd((blocks, piece, half), BF16)] + [halo_shape] * 2)
    fetched = flip(sent, "ch", 0)
    lo, hi = shift(ups, 1), shift(downs, -1)
    taps_other = flip(kernels, "ch", 0)

    def halo_plan(source, halo, skip, out, first, many):
        rows = pl.ds(skip, halo)
        return [
            (source, theirs(first, everything, many), out, (slice(None), everything)),
            (2, theirs(first, rows, many), out, (slice(None), pl.ds(bins, halo))),
            (3, theirs(first, rows, many), out, (slice(None), pl.ds(bins + halo, halo))),
        ]

    sent = pack(
        lambda: halo_plan(0, HX, 0, 0, 0, seqs) + [p for q in range(seqs) for p in halo_plan(1, HE, HX, 1 + q, q, 1)],
        3 + 3 * seqs,
        [inputs, cotangent, lo, hi],
        [sd((seqs, bins + 2 * HX, half), BF16)] + [sd((1, bins + 2 * HE, half), BF16)] * seqs,
    )
    inputs_sent, cot_sent = sent[0], sent[1:]

    marks = []
    orders = [list(range(share_bits - 1, 0, -1)) if b % 2 == 0 else list(range(1, share_bits)) for b in range(blocks)]
    for b in range(blocks):
        own_marks = [0]
        for bit in orders[b]:
            own_marks = own_marks + [mark ^ (1 << bit) for mark in own_marks]
        marks.append(tuple(own_marks + [mark ^ 1 for mark in own_marks]))
    early, last_bits = [order[:-1] for order in orders], [order[-1] for order in orders]

    fetched, inputs_sent, taps_other = join(fetched, inputs_sent, taps_other)
    held = [fetched[b : b + 1] for b in range(blocks)]
    inputs_other = flip(inputs_sent, "ch", 0)
    got = [flip(held[b], "seq", bit) for b in range(2) for bit in early[b]]
    token = fence(fetched[0, :16, :128], inputs_sent)
    token, *got = join(token, *got)
    if got:
        held[:2] = [jnp.concatenate([held[b], got[b]]) for b in range(2)]

    got = [flip(held[b], "seq", last_bits[b]) for b in range(2)]
    token, held[2], cot_first = join(token, held[2], cot_sent[0])
    got2 = [flip(held[2], "seq", bit) for bit in early[2]]
    cot_other = [flip(cot_first, "ch", 0)]
    token, inputs_other, cot_other[0], *got = join(token, inputs_other, cot_other[0], *got, *got2)
    near, far = [None] * blocks, [None] * blocks
    for b in range(2):
        near[b] = jnp.concatenate([held[b], got[b]])
        far[b] = flip(near[b], "seq", 0)
    held[2] = jnp.concatenate([held[2], *got[2:]])
    got2 = flip(held[2], "seq", last_bits[2])
    token, *sent = join(token, *cot_sent[1:])
    cot_other += [flip(c, "ch", 0) for c in sent]

    rows_x, rows_e = bins + 2 * HX, bins + 2 * HE
    weight_scratch = [pltpu.VMEM((2, chans, half), BF16), pltpu.SemaphoreType.DMA((2 + parts,))]
    act_shape, slope_shape = sd((seqs, bins, chans), BF16), sd((seqs, rows_e, chans), BF16)
    acts_scratch = pltpu.VMEM((seqs, rows_x, chans), BF16)
    taps = [kernels, taps_other]
    current = None
    saved = []
    for b in range(blocks - 1):
        scratch = [acts_scratch] + weight_scratch
        if b == 0:
            lead, specs = [inputs, lo, hi, inputs_other], [ANY] * 4
            scratch = scratch + [acts_scratch, pltpu.SemaphoreType.DMA((6 * seqs,))]
        else:
            lead, specs = [current], [VMEM]
        current, act, slope = call(
            functools.partial(forward_kernel, b, b == 0, marks[b]),
            specs + [VMEM, VMEM, ANY, ANY, ANY],
            [sd((seqs, rows_x, chans), BF16), act_shape, slope_shape],
            scratch,
            8,
        )(*lead, *taps, mixers, near[b], far[b])
        saved.append((act, slope))
        if b == 0:
            current, far[1], *cot_other = join(current, far[1], *cot_other)
        else:
            current, got2 = join(current, got2)
            near[2] = jnp.concatenate([held[2], got2])
            far[2] = flip(near[2], "seq", 0)

    def both(own, received):
        many = seqs // len(received)

        def plan():
            return [(0, slice(None), 0, ours(0, everything))] + [
                (1 + i, slice(None), 0, theirs(i * many, everything, many)) for i in range(len(received))
            ]

        return pack(plan, 1 + len(received), [own, *received, token], [sd(inputs.shape, BF16)])[0]

    scale = 1.0 / math.sqrt(all_seqs * bins * n)
    count = n
    size = chans // n
    turned = pltpu.VMEM((count, size, seqs * bins), BF16 if size % 16 == 0 else F32)
    shares = [sd((2, count // 2, size, half), BF16)] * 2

    class Exchange:
        def __init__(self, keep, send, order):
            shape = (2,) * bits + (size, half)
            self.pieces = [keep.reshape(shape), flip(send, "seq", 0).reshape(shape)]
            self.dims = ["ch"] + list(range(bits - 1, 0, -1))
            self.order = list(order)

        def arrived(self, token):
            token, self.pieces[-1] = join(token, self.pieces[-1])
            return token

        def step(self):
            axis = self.order.pop(0)
            at = self.dims.index(axis)
            self.dims.pop(at)
            sent = sum(lax.index_in_dim(p, 1, at, keepdims=False).astype(F32) for p in self.pieces).astype(BF16)
            kept = [lax.index_in_dim(p, 0, at, keepdims=False) for p in self.pieces]
            self.pieces = kept + [flip(sent, "ch", 0) if axis == "ch" else flip(sent, "seq", axis)]
            return sent

        def result(self):
            return sum(p.astype(F32) for p in self.pieces)

    if bits == 4:
        orders = [["ch", 1, 2, 3], [1, 2, "ch", 3], [2, 1, "ch", 3]]
    else:
        orders = [list(range(1, bits)) + ["ch"]] * blocks

    top = blocks - 1
    got = call(
        functools.partial(turn_kernel, top, scale),
        [VMEM] + [ANY] * 5 + [VMEM] * 2,
        [act_shape, slope_shape, slope_shape] + shares,
        [turned, pltpu.SemaphoreType.DMA((6 * seqs,))],
        8,
    )(current, cotangent, lo, hi, *cot_other, *taps)
    act, slope, upper, keep, send = got
    saved.append((act, slope))
    act, far[2] = join(act, far[2])
    exchanges = [None] * blocks
    exchanges[top] = Exchange(keep, send, orders[top])
    one_shape = sd((1, bins, half), BF16)
    for b in range(top, -1, -1):
        weights = [*taps, mixers, near[b], far[b]]
        slope = saved[b][1]
        scratch = weight_scratch
        if b == top:
            lead, outs = [current, act, upper, slope], [seqs_shape] + [one_shape] * seqs + [slope_shape]
        elif b:
            lead, outs = [upper, slope, saved[b][0]], [slope_shape] + shares
            scratch = scratch + [turned]
        else:
            lead, outs = [upper, slope], [seqs_shape] * 2
        got = call(
            functools.partial(backward_kernel, b, b == top, b == 0, marks[b], scale),
            [VMEM] * (len(lead) + 2) + [ANY, ANY, ANY],
            outs,
            scratch,
            8 if b == top else 6,
        )(*lead, *weights)
        if b == top:
            out_own, *out_sent, upper = got
            upper, exchanges[b].pieces[-1] = join(upper, exchanges[b].pieces[-1])
            out_received = [flip(out_sent[0], "ch", 0)]
        elif b:
            upper, keep, send = got
            exchanges[b] = Exchange(keep, send, orders[b])
            upper, out_received[0] = join(upper, out_received[0])
        else:
            in_own, in_sent = got
        if b == 1:
            keep, send = call(
                functools.partial(gradient_kernel, scale),
                [VMEM] * 2,
                shares,
                [turned],
                4,
            )(saved[0][0], upper)
            exchanges[0] = Exchange(keep, send, orders[0])
            keep, exchanges[1].pieces[-1] = join(keep, exchanges[1].pieces[-1])
            exchanges[0].pieces[0] = keep.reshape(exchanges[0].pieces[0].shape)
            for e in exchanges[:0:-1]:
                e.step()
            out_received += [flip(sent, "ch", 0) for sent in out_sent[1:]]
    in_own, *out_received = join(in_own, *out_received)
    token = fence(token, in_own)
    token = exchanges[0].arrived(token)
    token = fence(token, exchanges[0].step())
    in_received = None
    while any(e.order for e in exchanges):
        for e in exchanges[::-1]:
            if e.order:
                token = fence(e.arrived(token), e.step())
        if in_received is None:
            token, in_sent = join(token, in_sent)
            in_received = flip(in_sent, "ch", 0)
            token = fence(token, in_sent)
    for e in exchanges:
        token = e.arrived(token)
    token, in_received = join(token, in_received)
    grads = [e.result() for e in exchanges]
    return both(out_own, out_received), both(in_own, [in_received]), jnp.stack(grads)


def solution(mesh):
    placed = (P(None, "seq", "ch"), P(None, None, "ch"), P(None, None, "ch"), P(None, "seq", "ch"))
    return jax.shard_map(
        on_device,
        mesh=mesh,
        in_specs=placed,
        out_specs=(P(None, "seq", "ch"), P(None, "seq", "ch"), P(None, "seq", "ch")),
        check_vma=False,
    )
```

```python
import functools
import math

import jax
import jax.numpy as jnp
from jax import lax
from jax.experimental import pallas as pl
from jax.experimental.pallas import tpu as pltpu
from jax.sharding import PartitionSpec as P

DILATIONS = (2, 4, 8)
HX = 32
HE = 16
TILE = 256
BF16, F32 = jnp.bfloat16, jnp.float32
VMEM_BYTES = 28 * 1024 * 1024


def flip(value, axis, bit):
    count = lax.axis_size(axis)
    return lax.ppermute(value, axis, [(i, i ^ (1 << bit)) for i in range(count)])


def shift(value, step):
    count = lax.axis_size("seq")
    return lax.ppermute(value, "seq", [(i, i + step) for i in range(count) if 0 <= i + step < count])


def start_all(copies):
    for copy in copies:
        copy.start()


def wait_all(copies):
    for copy in copies:
        copy.wait()


def weight_copies(mix, near, far, weights, sems, block, marks):
    c = lax.axis_index("ch")
    half = mix.shape[1] // 2
    size = near.shape[1]
    per_half = half // size
    parts = 2 * near.shape[0]
    part = lax.axis_index("seq") % parts
    copies = []
    for h in range(2):
        copies.append(
            pltpu.make_async_copy(
                mix.at[block, pl.ds(pl.multiple_of((h ^ c) * half, half), half), :],
                weights.at[0, pl.ds(h * half, half), :],
                sems.at[h],
            )
        )
    for rel in range(parts):
        source = near if rel < parts // 2 else far
        place = part ^ marks[rel]
        row = ((place // per_half) ^ c) * half + (place % per_half) * size
        copies.append(
            pltpu.make_async_copy(
                source.at[rel % (parts // 2)],
                weights.at[1, pl.ds(pl.multiple_of(row, size), size), :],
                sems.at[2 + rel],
            )
        )
    return copies


def gather_copies(own, lo_own, hi_own, partner, buffer, sems, halo, skip):
    c = lax.axis_index("ch")
    seqs = buffer.shape[0]
    bins, half = own.shape[1:]
    low, main, high = pl.ds(0, halo), pl.ds(halo, bins), pl.ds(halo + bins, halo)
    cols = [pl.ds(side * half, half) for side in range(2)]
    pieces = []
    for q in range(seqs):
        at = c * seqs + q
        pieces.append((own.at[at], buffer.at[q, main, cols[0]]))
        pieces.append((lo_own.at[at, pl.ds(skip, halo), :], buffer.at[q, low, cols[0]]))
        pieces.append((hi_own.at[at, pl.ds(skip, halo), :], buffer.at[q, high, cols[0]]))
        other, row = (partner, q) if not isinstance(partner, (list, tuple)) else (partner[q], 0)
        pieces.append((other.at[row, pl.ds(0, bins), :], buffer.at[q, main, cols[1]]))
        pieces.append((other.at[row, pl.ds(bins, halo), :], buffer.at[q, low, cols[1]]))
        pieces.append((other.at[row, pl.ds(bins + halo, halo), :], buffer.at[q, high, cols[1]]))
    return [pltpu.make_async_copy(a, b, sems.at[i]) for i, (a, b) in enumerate(pieces)]


def taps_of(taps, block, tile):
    side, at = divmod(tile * TILE, taps[0].shape[2])
    return [taps[side][block, k : k + 1, at : at + TILE] for k in range(3)]


def activations(block, taps, current, q, tile, keep_rows):
    rows = current.shape[1]
    width = DILATIONS[block]
    cols = slice(tile * TILE, (tile + 1) * TILE)
    k0, k1, k2 = taps_of(taps, block, tile)
    wide = current[q, :, cols].astype(F32)
    pre = k0 * pltpu.roll(wide, width, 0) + k1 * wide + k2 * pltpu.roll(wide, rows - width, 0)
    pre = pre[keep_rows]
    cdf = 0.5 * (1.0 + lax.erf(pre * 0.7071067811865476))
    slope = cdf + pre * jnp.exp(-0.5 * pre * pre) * 0.3989422804014327
    return (pre * cdf).astype(BF16), slope.astype(BF16)


def zero_outside(array, halo):
    seqs, rows, chans = array.shape
    at = lax.axis_index("seq")

    @pl.when(at == 0)
    def _():
        array[:, 0:halo, :] = jnp.zeros((seqs, halo, chans), BF16)

    @pl.when(at == lax.axis_size("seq") - 1)
    def _():
        array[:, rows - halo : rows, :] = jnp.zeros((seqs, halo, chans), BF16)


def mix_tile(acts, weights, tile):
    half = weights.shape[2]
    side, at = divmod(tile * TILE, half)
    return jnp.dot(acts, weights[side, :, at : at + TILE], preferred_element_type=F32)


def forward_kernel(block, first, marks, *refs):
    if first:
        own, lo, hi, partner, t0, t1, mix, near, far, nxt, act_out, slope_out, acts, weights, wsems, current, sems = refs
        loads = gather_copies(own, lo, hi, partner, current, sems, HX, 0)
    else:
        current, t0, t1, mix, near, far, nxt, act_out, slope_out, acts, weights, wsems = refs
        loads = []
    brings = weight_copies(mix, near, far, weights, wsems, block, marks)
    start_all(loads)
    start_all(brings)
    wait_all(loads)
    seqs, rows, chans = current.shape
    bins = rows - 2 * HX
    edge = HX - HE
    for q in range(seqs):
        for tile in range(chans // TILE):
            cols = slice(tile * TILE, (tile + 1) * TILE)
            act, slope = activations(block, (t0, t1), current, q, tile, slice(None))
            slope_out[q, :, cols] = slope[edge : rows - edge]
            acts[q, :, cols] = act
            act_out[q, :, cols] = act[HX : HX + bins]
    wait_all(brings)
    for tile in range(chans // TILE):
        cols = slice(tile * TILE, (tile + 1) * TILE)
        for q in range(seqs):
            nxt[q, :, cols] = (current[q, :, cols].astype(F32) + mix_tile(acts[q], weights, tile)).astype(BF16)
    zero_outside(nxt, HX)


def gradient(act, upper, turned, keep, send, scale):
    seqs, bins, chans = act.shape
    half = chans // 2
    c, s = lax.axis_index("ch"), lax.axis_index("seq")
    count, size, _ = turned.shape
    for h in range(2):
        for q in range(seqs):
            flat = act[q, :, h * half : (h + 1) * half].T.astype(turned.dtype)
            for i in range(count // 2):
                rel = ((h ^ c) * (count // 2) + i) ^ s
                place = (rel & 1) * (count // 2) + (rel >> 1)
                turned[place, :, q * bins : (q + 1) * bins] = flat[i * size : (i + 1) * size]
    for part, target in enumerate((keep, send)):
        first_row = part * (count // 2)
        left = turned[first_row : first_row + count // 2].reshape(count // 2 * size, seqs * bins).astype(BF16)
        for tile in range(chans // TILE):
            cols = slice(tile * TILE, (tile + 1) * TILE)
            side, at = divmod(tile * TILE, half)
            total = sum(
                jnp.dot(left[:, q * bins : (q + 1) * bins], upper[q, HE : HE + bins, cols], preferred_element_type=F32)
                for q in range(seqs)
            )
            total = (total * scale).reshape(count // 2, size, TILE)
            target[side, :, :, at : at + TILE] = total.astype(BF16)


def turn_kernel(block, scale, *refs):
    current, own, lo, hi, p0, p1, t0, t1, act, slope_out, upper, keep, send, turned, sems = refs
    loads = gather_copies(own, lo, hi, (p0, p1), upper, sems, HE, HX)
    start_all(loads)
    seqs, rows, chans = current.shape
    edge = HX - HE
    for q in range(seqs):
        for tile in range(chans // TILE):
            cols = slice(tile * TILE, (tile + 1) * TILE)
            value, slope = activations(block, (t0, t1), current, q, tile, slice(edge, rows - edge))
            slope_out[q, :, cols] = slope
            act[q, :, cols] = value[HE : HE + act.shape[1]]
    wait_all(loads)
    gradient(act, upper, turned, keep, send, scale)


def gradient_kernel(scale, act, upper, keep, send, turned):
    gradient(act, upper, turned, keep, send, scale)


def output_kernel(block, marks, current, act, mix, near, far, out, *refs):
    out_others, weights, wsems = refs[:-2], refs[-2], refs[-1]
    brings = weight_copies(mix, near, far, weights, wsems, block, marks)
    start_all(brings)
    wait_all(brings)
    seqs, bins, chans = act.shape
    half = chans // 2
    for tile in range(chans // TILE):
        cols = slice(tile * TILE, (tile + 1) * TILE)
        side, at = divmod(tile * TILE, half)
        for q in range(seqs):
            value = (current[q, HX : HX + bins, cols].astype(F32) + mix_tile(act[q], weights, tile)).astype(BF16)
            if side:
                out_others[q][0, :, at : at + TILE] = value
            else:
                out[q, :, at : at + TILE] = value


def backward_kernel(block, top, last, marks, scale, *refs):
    if top:
        upper, slopes, t0, t1, mix, near, far, lower, weights, wsems = refs
    elif last:
        upper, slopes, t0, t1, mix, near, far, lower, lower_other, weights, wsems = refs
    else:
        upper, slopes, act, t0, t1, mix, near, far, lower, keep, send, weights, wsems, turned = refs
    brings = weight_copies(mix, near, far, weights, wsems, block, marks)
    start_all(brings)
    if not top and not last:
        gradient(act, upper, turned, keep, send, scale)
    wait_all(brings)
    seqs, rows, chans = upper.shape
    half = chans // 2
    width = DILATIONS[block]
    bins = rows - 2 * HE
    for q in range(seqs):
        for tile in range(chans // TILE):
            cols = slice(tile * TILE, (tile + 1) * TILE)
            side, at = divmod(tile * TILE, half)
            back = sum(
                lax.dot_general(
                    upper[q, :, g * half : (g + 1) * half],
                    weights[g, cols, :],
                    (((1,), (1,)), ((), ())),
                    preferred_element_type=F32,
                )
                for g in range(2)
            )
            slope = (back * slopes[q, :, cols].astype(F32)).astype(BF16).astype(F32)
            k0, k1, k2 = taps_of((t0, t1), block, tile)
            new = upper[q, :, cols].astype(F32) + k0 * pltpu.roll(slope, rows - width, 0) + k1 * slope + k2 * pltpu.roll(slope, width, 0)
            new = new.astype(BF16)
            if last:
                (lower, lower_other)[side][q, :, at : at + TILE] = new[HE : HE + bins]
            else:
                lower[q, :, cols] = new
    if not last:
        zero_outside(lower, HE)


ANY = pl.BlockSpec(memory_space=pl.ANY)
VMEM = pl.BlockSpec(memory_space=pltpu.VMEM)


def call(kernel, in_specs, outs, scratch, micros, out_specs=None):
    return pl.pallas_call(
        kernel,
        in_specs=in_specs,
        out_specs=out_specs or [VMEM] * len(outs),
        out_shape=outs,
        scratch_shapes=scratch,
        compiler_params=pltpu.CompilerParams(vmem_limit_bytes=VMEM_BYTES),
        cost_estimate=pl.CostEstimate(flops=int(micros * 1.15e9), bytes_accessed=int(micros * 3.6e6), transcendentals=0),
    )


def pack_kernel(plan, operands, *refs):
    ins, outs, sems = refs[:operands], refs[operands:-1], refs[-1]
    copies = [
        pltpu.make_async_copy(ins[i].at[src], outs[o].at[dst], sems.at[k])
        for k, (i, src, o, dst) in enumerate(plan())
    ]
    start_all(copies)
    wait_all(copies)


def in_hbm(value):
    return pltpu.with_memory_space_constraint(value, pltpu.HBM)


def pack(plan, count, operands, outs):
    return call(
        functools.partial(pack_kernel, plan, len(operands)),
        [ANY] * len(operands),
        outs,
        [pltpu.SemaphoreType.DMA((count,))],
        1,
    )(*operands)


def fence_kernel(token, *refs):
    refs[-1][...] = token[...]


def fence(token, *others):
    return call(
        fence_kernel,
        [VMEM] + [ANY] * len(others),
        [jax.ShapeDtypeStruct(token.shape, token.dtype)],
        [],
        1,
    )(token, *others)[0]


def join(*values):
    return lax.optimization_barrier(values)


def on_device(inputs, kernels, mixers, cotangent):
    all_seqs, bins, half = inputs.shape
    n, m = lax.axis_size("seq"), lax.axis_size("ch")
    seqs, chans = all_seqs // m, half * m
    bits = n.bit_length() - 1
    blocks = mixers.shape[0]
    share_bits = min(3, bits)
    parts = 1 << share_bits
    piece = chans // parts
    sd = jax.ShapeDtypeStruct

    def ours(first, rows):
        return (pl.ds(lax.axis_index("ch") * seqs + first, seqs - first), rows)

    def theirs(first, rows, many=seqs):
        return (pl.ds((1 - lax.axis_index("ch")) * seqs + first, many), rows)

    everything = pl.ds(0, bins)
    inputs, cotangent, mixers = in_hbm(inputs), in_hbm(cotangent), in_hbm(mixers)

    def first_plan():
        plan = []
        for b in range(blocks):
            piece_rows = pl.ds(pl.multiple_of(lax.axis_index("seq") % parts * piece, piece), piece)
            plan.append((2, (b, piece_rows), 0, b))
        for place, (rows_x, rows_e) in enumerate(((pl.ds(bins - HX, HX), pl.ds(bins - HE, HE)), (pl.ds(0, HX), pl.ds(0, HE)))):
            plan.append((0, (slice(None), rows_x), 1 + place, (slice(None), pl.ds(0, HX))))
            plan.append((1, (slice(None), rows_e), 1 + place, (slice(None), pl.ds(HX, HE))))
        return plan

    seqs_shape = sd((seqs, bins, half), BF16)
    halo_shape = sd((all_seqs, HX + HE, half), BF16)
    sent, ups, downs = pack(first_plan, blocks + 4, [inputs, cotangent, mixers], [sd((blocks, piece, half), BF16)] + [halo_shape] * 2)
    fetched = flip(sent, "ch", 0)
    lo, hi = shift(ups, 1), shift(downs, -1)
    taps_other = flip(kernels, "ch", 0)

    def halo_plan(source, halo, skip, out, first, many):
        rows = pl.ds(skip, halo)
        return [
            (source, theirs(first, everything, many), out, (slice(None), everything)),
            (2, theirs(first, rows, many), out, (slice(None), pl.ds(bins, halo))),
            (3, theirs(first, rows, many), out, (slice(None), pl.ds(bins + halo, halo))),
        ]

    sent = pack(
        lambda: halo_plan(0, HX, 0, 0, 0, seqs) + [p for q in range(seqs) for p in halo_plan(1, HE, HX, 1 + q, q, 1)],
        3 + 3 * seqs,
        [inputs, cotangent, lo, hi],
        [sd((seqs, bins + 2 * HX, half), BF16)] + [sd((1, bins + 2 * HE, half), BF16)] * seqs,
    )
    inputs_sent, cot_sent = sent[0], sent[1:]

    marks = []
    orders = [list(range(share_bits - 1, 0, -1)) if b % 2 == 0 else list(range(1, share_bits)) for b in range(blocks)]
    for b in range(blocks):
        own_marks = [0]
        for bit in orders[b]:
            own_marks = own_marks + [mark ^ (1 << bit) for mark in own_marks]
        marks.append(tuple(own_marks + [mark ^ 1 for mark in own_marks]))
    early, last_bits = [order[:-1] for order in orders], [order[-1] for order in orders]

    fetched, inputs_sent, taps_other = join(fetched, inputs_sent, taps_other)
    held = [fetched[b : b + 1] for b in range(blocks)]
    inputs_other = flip(inputs_sent, "ch", 0)
    got = [flip(held[b], "seq", bit) for b in range(2) for bit in early[b]]
    token = fence(fetched[0, :16, :128], inputs_sent)
    token, *got = join(token, *got)
    if got:
        held[:2] = [jnp.concatenate([held[b], got[b]]) for b in range(2)]

    got = [flip(held[b], "seq", last_bits[b]) for b in range(2)]
    token, held[2], cot_first = join(token, held[2], cot_sent[0])
    got2 = [flip(held[2], "seq", bit) for bit in early[2]]
    token, inputs_other, *got = join(token, inputs_other, *got, *got2)
    cot_other = [flip(cot_first, "ch", 0)]
    near, far = [None] * blocks, [None] * blocks
    for b in range(2):
        near[b] = jnp.concatenate([held[b], got[b]])
        far[b] = flip(near[b], "seq", 0)
    held[2] = jnp.concatenate([held[2], *got[2:]])
    got2 = flip(held[2], "seq", last_bits[2])
    token, *sent = join(token, *cot_sent[1:])
    cot_other += [flip(c, "ch", 0) for c in sent]

    rows_x, rows_e = bins + 2 * HX, bins + 2 * HE
    weight_scratch = [pltpu.VMEM((2, chans, half), BF16), pltpu.SemaphoreType.DMA((2 + parts,))]
    act_shape, slope_shape = sd((seqs, bins, chans), BF16), sd((seqs, rows_e, chans), BF16)
    acts_scratch = pltpu.VMEM((seqs, rows_x, chans), BF16)
    taps = [kernels, taps_other]
    current = None
    saved = []
    for b in range(blocks - 1):
        scratch = [acts_scratch] + weight_scratch
        if b == 0:
            lead, specs = [inputs, lo, hi, inputs_other], [ANY] * 4
            scratch = scratch + [acts_scratch, pltpu.SemaphoreType.DMA((6 * seqs,))]
        else:
            lead, specs = [current], [VMEM]
        current, act, slope = call(
            functools.partial(forward_kernel, b, b == 0, marks[b]),
            specs + [VMEM, VMEM, ANY, ANY, ANY],
            [sd((seqs, rows_x, chans), BF16), act_shape, slope_shape],
            scratch,
            8,
        )(*lead, *taps, mixers, near[b], far[b])
        saved.append((act, slope))
        if b == 0:
            current, far[1], cot_other[0] = join(current, far[1], cot_other[0])
        else:
            current, got2, *cot_other[1:] = join(current, got2, *cot_other[1:])
            near[2] = jnp.concatenate([held[2], got2])
            far[2] = flip(near[2], "seq", 0)

    def both(own, received):
        many = seqs // len(received)

        def plan():
            return [(0, slice(None), 0, ours(0, everything))] + [
                (1 + i, slice(None), 0, theirs(i * many, everything, many)) for i in range(len(received))
            ]

        return pack(plan, 1 + len(received), [own, *received, token], [sd(inputs.shape, BF16)])[0]

    scale = 1.0 / math.sqrt(all_seqs * bins * n)
    count = n
    size = chans // n
    turned = pltpu.VMEM((count, size, seqs * bins), BF16 if size % 16 == 0 else F32)
    shares = [sd((2, count // 2, size, half), BF16)] * 2

    class Exchange:
        def __init__(self, keep, send, order):
            shape = (2,) * bits + (size, half)
            self.pieces = [keep.reshape(shape), flip(send, "seq", 0).reshape(shape)]
            self.dims = ["ch"] + list(range(bits - 1, 0, -1))
            self.order = list(order)

        def arrived(self, token):
            token, self.pieces[-1] = join(token, self.pieces[-1])
            return token

        def step(self):
            axis = self.order.pop(0)
            at = self.dims.index(axis)
            self.dims.pop(at)
            sent = sum(lax.index_in_dim(p, 1, at, keepdims=False).astype(F32) for p in self.pieces).astype(BF16)
            kept = [lax.index_in_dim(p, 0, at, keepdims=False) for p in self.pieces]
            self.pieces = kept + [flip(sent, "ch", 0) if axis == "ch" else flip(sent, "seq", axis)]
            return sent

        def result(self):
            return sum(p.astype(F32) for p in self.pieces)

    if bits == 4:
        orders = [["ch", 1, 2, 3], [1, 2, "ch", 3], [2, 1, "ch", 3]]
    else:
        orders = [list(range(1, bits)) + ["ch"]] * blocks

    top = blocks - 1
    got = call(
        functools.partial(turn_kernel, top, scale),
        [VMEM] + [ANY] * 5 + [VMEM] * 2,
        [act_shape, slope_shape, slope_shape] + shares,
        [turned, pltpu.SemaphoreType.DMA((6 * seqs,))],
        8,
    )(current, cotangent, lo, hi, *cot_other, *taps)
    act, slope, upper, keep, send = got
    saved.append((act, slope))
    act, far[2], send = join(act, far[2], send)
    exchanges = [None] * blocks
    exchanges[top] = Exchange(keep, send, orders[top])
    one_shape = sd((1, bins, half), BF16)
    for b in range(top, -1, -1):
        weights = [*taps, mixers, near[b], far[b]]
        slope = saved[b][1]
        scratch = weight_scratch
        if b == top:
            out_own, *out_sent = call(
                functools.partial(output_kernel, b, marks[b]),
                [VMEM, VMEM, ANY, ANY, ANY],
                [seqs_shape] + [one_shape] * seqs,
                weight_scratch,
                4,
            )(current, act, mixers, near[b], far[b])
            out_received = [flip(out_sent[0], "ch", 0)]
            upper, out_own = join(upper, out_own)
            lead, outs = [upper, slope], [slope_shape]
        elif b:
            lead, outs = [upper, slope, saved[b][0]], [slope_shape] + shares
            scratch = scratch + [turned]
        else:
            lead, outs = [upper, slope], [seqs_shape] * 2
        got = call(
            functools.partial(backward_kernel, b, b == top, b == 0, marks[b], scale),
            [VMEM] * (len(lead) + 2) + [ANY, ANY, ANY],
            outs,
            scratch,
            8 if b == top else 6,
        )(*lead, *weights)
        if b == top:
            upper = got[0]
            upper, exchanges[b].pieces[-1], out_received[0] = join(upper, exchanges[b].pieces[-1], out_received[0])
            out_received += [flip(sent, "ch", 0) for sent in out_sent[1:]]
        elif b:
            upper, keep, send = got
            exchanges[b] = Exchange(keep, send, orders[b])
            upper, *out_received[1:] = join(upper, *out_received[1:])
        else:
            in_own, in_sent = got
        if b == 1:
            keep, send = call(
                functools.partial(gradient_kernel, scale),
                [VMEM] * 2,
                shares,
                [turned],
                4,
            )(saved[0][0], upper)
            exchanges[0] = Exchange(keep, send, orders[0])
            keep, exchanges[1].pieces[-1] = join(keep, exchanges[1].pieces[-1])
            exchanges[0].pieces[0] = keep.reshape(exchanges[0].pieces[0].shape)
            for e in exchanges[:0:-1]:
                e.step()
    token = fence(token, in_own)
    token = exchanges[0].arrived(token)
    token = fence(token, exchanges[0].step())
    in_received = None
    while any(e.order for e in exchanges):
        for e in exchanges[::-1]:
            if e.order:
                token = fence(e.arrived(token), e.step())
        if in_received is None:
            token, in_sent = join(token, in_sent)
            in_received = flip(in_sent, "ch", 0)
            token = fence(token, in_sent)
    for e in exchanges:
        token = e.arrived(token)
    token, in_received = join(token, in_received)
    grads = [e.result() for e in exchanges]
    return both(out_own, out_received), both(in_own, [in_received]), jnp.stack(grads)


def solution(mesh):
    placed = (P(None, "seq", "ch"), P(None, None, "ch"), P(None, None, "ch"), P(None, "seq", "ch"))
    return jax.shard_map(
        on_device,
        mesh=mesh,
        in_specs=placed,
        out_specs=(P(None, "seq", "ch"), P(None, "seq", "ch"), P(None, "seq", "ch")),
        check_vma=False,
    )
```

```python
import functools
import math

import jax
import jax.numpy as jnp
from jax import lax
from jax.experimental import pallas as pl
from jax.experimental.pallas import tpu as pltpu
from jax.sharding import PartitionSpec as P

DILATIONS = (2, 4, 8)
HX = 32
HE = 16
TILE = 256
BF16, F32 = jnp.bfloat16, jnp.float32
VMEM_BYTES = 28 * 1024 * 1024


def flip(value, axis, bit):
    count = lax.axis_size(axis)
    return lax.ppermute(value, axis, [(i, i ^ (1 << bit)) for i in range(count)])


def shift(value, step):
    count = lax.axis_size("seq")
    return lax.ppermute(value, "seq", [(i, i + step) for i in range(count) if 0 <= i + step < count])


def start_all(copies):
    for copy in copies:
        copy.start()


def wait_all(copies):
    for copy in copies:
        copy.wait()


def weight_copies(mix, near, far, weights, sems, block, marks):
    c = lax.axis_index("ch")
    half = mix.shape[1] // 2
    size = near.shape[1]
    per_half = half // size
    parts = 2 * near.shape[0]
    part = lax.axis_index("seq") % parts
    copies = []
    for h in range(2):
        copies.append(
            pltpu.make_async_copy(
                mix.at[block, pl.ds(pl.multiple_of((h ^ c) * half, half), half), :],
                weights.at[0, pl.ds(h * half, half), :],
                sems.at[h],
            )
        )
    for rel in range(parts):
        source = near if rel < parts // 2 else far
        place = part ^ marks[rel]
        row = ((place // per_half) ^ c) * half + (place % per_half) * size
        copies.append(
            pltpu.make_async_copy(
                source.at[rel % (parts // 2)],
                weights.at[1, pl.ds(pl.multiple_of(row, size), size), :],
                sems.at[2 + rel],
            )
        )
    return copies


def gather_copies(own, lo_own, hi_own, partner, buffer, sems, halo, skip):
    c = lax.axis_index("ch")
    seqs = buffer.shape[0]
    bins, half = own.shape[1:]
    low, main, high = pl.ds(0, halo), pl.ds(halo, bins), pl.ds(halo + bins, halo)
    cols = [pl.ds(side * half, half) for side in range(2)]
    pieces = []
    for q in range(seqs):
        at = c * seqs + q
        pieces.append((own.at[at], buffer.at[q, main, cols[0]]))
        pieces.append((lo_own.at[at, pl.ds(skip, halo), :], buffer.at[q, low, cols[0]]))
        pieces.append((hi_own.at[at, pl.ds(skip, halo), :], buffer.at[q, high, cols[0]]))
        other, row = (partner, q) if not isinstance(partner, (list, tuple)) else (partner[q], 0)
        pieces.append((other.at[row, pl.ds(0, bins), :], buffer.at[q, main, cols[1]]))
        pieces.append((other.at[row, pl.ds(bins, halo), :], buffer.at[q, low, cols[1]]))
        pieces.append((other.at[row, pl.ds(bins + halo, halo), :], buffer.at[q, high, cols[1]]))
    return [pltpu.make_async_copy(a, b, sems.at[i]) for i, (a, b) in enumerate(pieces)]


def taps_of(taps, block, tile):
    side, at = divmod(tile * TILE, taps[0].shape[2])
    return [taps[side][block, k : k + 1, at : at + TILE] for k in range(3)]


def activations(block, taps, current, q, tile, keep_rows):
    rows = current.shape[1]
    width = DILATIONS[block]
    cols = slice(tile * TILE, (tile + 1) * TILE)
    k0, k1, k2 = taps_of(taps, block, tile)
    wide = current[q, :, cols].astype(F32)
    pre = k0 * pltpu.roll(wide, width, 0) + k1 * wide + k2 * pltpu.roll(wide, rows - width, 0)
    pre = pre[keep_rows]
    cdf = 0.5 * (1.0 + lax.erf(pre * 0.7071067811865476))
    slope = cdf + pre * jnp.exp(-0.5 * pre * pre) * 0.3989422804014327
    return (pre * cdf).astype(BF16), slope.astype(BF16)


def zero_outside(array, halo):
    seqs, rows, chans = array.shape
    at = lax.axis_index("seq")

    @pl.when(at == 0)
    def _():
        array[:, 0:halo, :] = jnp.zeros((seqs, halo, chans), BF16)

    @pl.when(at == lax.axis_size("seq") - 1)
    def _():
        array[:, rows - halo : rows, :] = jnp.zeros((seqs, halo, chans), BF16)


def mix_tile(acts, weights, tile):
    half = weights.shape[2]
    side, at = divmod(tile * TILE, half)
    return jnp.dot(acts, weights[side, :, at : at + TILE], preferred_element_type=F32)


def forward_kernel(block, first, marks, *refs):
    if first:
        own, lo, hi, partner, t0, t1, mix, near, far, nxt, act_out, slope_out, acts, weights, wsems, current, sems = refs
        loads = gather_copies(own, lo, hi, partner, current, sems, HX, 0)
    else:
        current, t0, t1, mix, near, far, nxt, act_out, slope_out, act_top, slope_top, acts, weights, wsems = refs
        loads = []
    brings = weight_copies(mix, near, far, weights, wsems, block, marks)
    start_all(loads)
    start_all(brings)
    wait_all(loads)
    seqs, rows, chans = current.shape
    bins = rows - 2 * HX
    edge = HX - HE
    for q in range(seqs):
        for tile in range(chans // TILE):
            cols = slice(tile * TILE, (tile + 1) * TILE)
            act, slope = activations(block, (t0, t1), current, q, tile, slice(None))
            slope_out[q, :, cols] = slope[edge : rows - edge]
            acts[q, :, cols] = act
            act_out[q, :, cols] = act[HX : HX + bins]
    wait_all(brings)
    for tile in range(chans // TILE):
        cols = slice(tile * TILE, (tile + 1) * TILE)
        for q in range(seqs):
            nxt[q, :, cols] = (current[q, :, cols].astype(F32) + mix_tile(acts[q], weights, tile)).astype(BF16)
    zero_outside(nxt, HX)
    if not first:
        for q in range(seqs):
            for tile in range(chans // TILE):
                cols = slice(tile * TILE, (tile + 1) * TILE)
                value, slope = activations(block + 1, (t0, t1), nxt, q, tile, slice(edge, rows - edge))
                slope_top[q, :, cols] = slope
                act_top[q, :, cols] = value[HE : HE + bins]


def gradient(act, upper, turned, keep, send, scale):
    seqs, bins, chans = act.shape
    half = chans // 2
    c, s = lax.axis_index("ch"), lax.axis_index("seq")
    count, size, _ = turned.shape
    for h in range(2):
        for q in range(seqs):
            flat = act[q, :, h * half : (h + 1) * half].T.astype(turned.dtype)
            for i in range(count // 2):
                rel = ((h ^ c) * (count // 2) + i) ^ s
                place = (rel & 1) * (count // 2) + (rel >> 1)
                turned[place, :, q * bins : (q + 1) * bins] = flat[i * size : (i + 1) * size]
    for part, target in enumerate((keep, send)):
        first_row = part * (count // 2)
        left = turned[first_row : first_row + count // 2].reshape(count // 2 * size, seqs * bins).astype(BF16)
        for tile in range(chans // TILE):
            cols = slice(tile * TILE, (tile + 1) * TILE)
            side, at = divmod(tile * TILE, half)
            total = sum(
                jnp.dot(left[:, q * bins : (q + 1) * bins], upper[q, HE : HE + bins, cols], preferred_element_type=F32)
                for q in range(seqs)
            )
            total = (total * scale).reshape(count // 2, size, TILE)
            target[side, :, :, at : at + TILE] = total.astype(BF16)


def turn_kernel(scale, act, own, lo, hi, p0, p1, upper, keep, send, turned, sems):
    loads = gather_copies(own, lo, hi, (p0, p1), upper, sems, HE, HX)
    start_all(loads)
    wait_all(loads)
    gradient(act, upper, turned, keep, send, scale)


def gradient_kernel(scale, act, upper, keep, send, turned):
    gradient(act, upper, turned, keep, send, scale)


def output_kernel(block, marks, current, act, mix, near, far, out, *refs):
    out_others, weights, wsems = refs[:-2], refs[-2], refs[-1]
    brings = weight_copies(mix, near, far, weights, wsems, block, marks)
    start_all(brings)
    wait_all(brings)
    seqs, bins, chans = act.shape
    half = chans // 2
    for tile in range(chans // TILE):
        cols = slice(tile * TILE, (tile + 1) * TILE)
        side, at = divmod(tile * TILE, half)
        for q in range(seqs):
            value = (current[q, HX : HX + bins, cols].astype(F32) + mix_tile(act[q], weights, tile)).astype(BF16)
            if side:
                out_others[q][0, :, at : at + TILE] = value
            else:
                out[q, :, at : at + TILE] = value


def backward_kernel(block, top, last, marks, scale, *refs):
    if top:
        upper, slopes, t0, t1, mix, near, far, lower, weights, wsems = refs
    elif last:
        upper, slopes, t0, t1, mix, near, far, lower, lower_other, weights, wsems = refs
    else:
        upper, slopes, act, t0, t1, mix, near, far, lower, keep, send, weights, wsems, turned = refs
    brings = weight_copies(mix, near, far, weights, wsems, block, marks)
    start_all(brings)
    if not top and not last:
        gradient(act, upper, turned, keep, send, scale)
    wait_all(brings)
    seqs, rows, chans = upper.shape
    half = chans // 2
    width = DILATIONS[block]
    bins = rows - 2 * HE
    for q in range(seqs):
        for tile in range(chans // TILE):
            cols = slice(tile * TILE, (tile + 1) * TILE)
            side, at = divmod(tile * TILE, half)
            back = sum(
                lax.dot_general(
                    upper[q, :, g * half : (g + 1) * half],
                    weights[g, cols, :],
                    (((1,), (1,)), ((), ())),
                    preferred_element_type=F32,
                )
                for g in range(2)
            )
            slope = (back * slopes[q, :, cols].astype(F32)).astype(BF16).astype(F32)
            k0, k1, k2 = taps_of((t0, t1), block, tile)
            new = upper[q, :, cols].astype(F32) + k0 * pltpu.roll(slope, rows - width, 0) + k1 * slope + k2 * pltpu.roll(slope, width, 0)
            new = new.astype(BF16)
            if last:
                (lower, lower_other)[side][q, :, at : at + TILE] = new[HE : HE + bins]
            else:
                lower[q, :, cols] = new
    if not last:
        zero_outside(lower, HE)


ANY = pl.BlockSpec(memory_space=pl.ANY)
VMEM = pl.BlockSpec(memory_space=pltpu.VMEM)


def call(kernel, in_specs, outs, scratch, micros, out_specs=None):
    return pl.pallas_call(
        kernel,
        in_specs=in_specs,
        out_specs=out_specs or [VMEM] * len(outs),
        out_shape=outs,
        scratch_shapes=scratch,
        compiler_params=pltpu.CompilerParams(vmem_limit_bytes=VMEM_BYTES),
        cost_estimate=pl.CostEstimate(flops=int(micros * 1.15e9), bytes_accessed=int(micros * 3.6e6), transcendentals=0),
    )


def pack_kernel(plan, operands, *refs):
    ins, outs, sems = refs[:operands], refs[operands:-1], refs[-1]
    copies = [
        pltpu.make_async_copy(ins[i].at[src], outs[o].at[dst], sems.at[k])
        for k, (i, src, o, dst) in enumerate(plan())
    ]
    start_all(copies)
    wait_all(copies)


def in_hbm(value):
    return pltpu.with_memory_space_constraint(value, pltpu.HBM)


def pack(plan, count, operands, outs):
    return call(
        functools.partial(pack_kernel, plan, len(operands)),
        [ANY] * len(operands),
        outs,
        [pltpu.SemaphoreType.DMA((count,))],
        1,
    )(*operands)


def fence_kernel(token, *refs):
    refs[-1][...] = token[...]


def fence(token, *others):
    return call(
        fence_kernel,
        [VMEM] + [ANY] * len(others),
        [jax.ShapeDtypeStruct(token.shape, token.dtype)],
        [],
        1,
    )(token, *others)[0]


def join(*values):
    return lax.optimization_barrier(values)


def on_device(inputs, kernels, mixers, cotangent):
    all_seqs, bins, half = inputs.shape
    n, m = lax.axis_size("seq"), lax.axis_size("ch")
    seqs, chans = all_seqs // m, half * m
    bits = n.bit_length() - 1
    blocks = mixers.shape[0]
    share_bits = min(3, bits)
    parts = 1 << share_bits
    piece = chans // parts
    sd = jax.ShapeDtypeStruct

    def ours(first, rows):
        return (pl.ds(lax.axis_index("ch") * seqs + first, seqs - first), rows)

    def theirs(first, rows, many=seqs):
        return (pl.ds((1 - lax.axis_index("ch")) * seqs + first, many), rows)

    def mixer_piece(b):
        return (b, pl.ds(pl.multiple_of(lax.axis_index("seq") % parts * piece, piece), piece))

    def third_rows(q):
        size = piece // seqs
        return pl.ds(pl.multiple_of(lax.axis_index("seq") % parts * piece + q * size, size), size)

    everything = pl.ds(0, bins)
    inputs, cotangent, mixers = in_hbm(inputs), in_hbm(cotangent), in_hbm(mixers)

    def first_plan():
        plan = []
        for b in range(2):
            plan.append((2, mixer_piece(b), 0, b))
        for place, (rows_x, rows_e) in enumerate(((pl.ds(bins - HX, HX), pl.ds(bins - HE, HE)), (pl.ds(0, HX), pl.ds(0, HE)))):
            plan.append((0, (slice(None), rows_x), 1 + place, (slice(None), pl.ds(0, HX))))
            plan.append((1, (slice(None), rows_e), 1 + place, (slice(None), pl.ds(HX, HE))))
        return plan

    seqs_shape = sd((seqs, bins, half), BF16)
    halo_shape = sd((all_seqs, HX + HE, half), BF16)
    sent, ups, downs = pack(first_plan, 6, [inputs, cotangent, mixers], [sd((2, piece, half), BF16)] + [halo_shape] * 2)
    fetched = flip(sent, "ch", 0)
    lo, hi = shift(ups, 1), shift(downs, -1)
    taps_other = flip(kernels, "ch", 0)

    def halo_plan(source, halo, skip, out, first, many):
        rows = pl.ds(skip, halo)
        return [
            (source, theirs(first, everything, many), out, (slice(None), everything)),
            (2, theirs(first, rows, many), out, (slice(None), pl.ds(bins, halo))),
            (3, theirs(first, rows, many), out, (slice(None), pl.ds(bins + halo, halo))),
        ]

    sent = pack(
        lambda: [(4, (2, third_rows(q)), 0, (q, pl.ds(bins + 2 * HX, piece // seqs))) for q in range(seqs)]
        + halo_plan(0, HX, 0, 0, 0, seqs)
        + [p for q in range(seqs) for p in halo_plan(1, HE, HX, 1 + q, q, 1)],
        3 + 4 * seqs,
        [inputs, cotangent, lo, hi, mixers],
        [sd((seqs, bins + 2 * HX + piece // seqs, half), BF16)] + [sd((1, bins + 2 * HE, half), BF16)] * seqs,
    )
    inputs_sent, cot_sent = sent[0], sent[1:]

    marks = []
    orders = [list(range(share_bits - 1, 0, -1)) if b % 2 == 0 else list(range(1, share_bits)) for b in range(blocks)]
    for b in range(blocks):
        own_marks = [0]
        for bit in orders[b]:
            own_marks = own_marks + [mark ^ (1 << bit) for mark in own_marks]
        marks.append(tuple(own_marks + [mark ^ 1 for mark in own_marks]))
    early, last_bits = [order[:-1] for order in orders], [order[-1] for order in orders]

    fetched, inputs_sent, taps_other = join(fetched, inputs_sent, taps_other)
    held = [fetched[b : b + 1] for b in range(2)]
    inputs_other = flip(inputs_sent, "ch", 0)
    got = [flip(held[b], "seq", bit) for b in range(2) for bit in early[b]]
    token = fence(fetched[0, :16, :128], inputs_sent)
    token, *got = join(token, *got)
    if got:
        held[:2] = [jnp.concatenate([held[b], got[b]]) for b in range(2)]

    got = [flip(held[b], "seq", last_bits[b]) for b in range(2)]
    token, inputs_other, *got = join(token, inputs_other, *got)
    near, far = [None] * blocks, [None] * blocks
    for b in range(2):
        near[b] = jnp.concatenate([held[b], got[b]])
        far[b] = flip(near[b], "seq", 0)
    held.append(inputs_other[:, bins + 2 * HX :].reshape(1, piece, half))
    third = [flip(held[2], "seq", bit) for bit in orders[2]]
    cot_other = [flip(c, "ch", 0) for c in cot_sent]

    rows_x, rows_e = bins + 2 * HX, bins + 2 * HE
    weight_scratch = [pltpu.VMEM((2, chans, half), BF16), pltpu.SemaphoreType.DMA((2 + parts,))]
    act_shape, slope_shape = sd((seqs, bins, chans), BF16), sd((seqs, rows_e, chans), BF16)
    acts_scratch = pltpu.VMEM((seqs, rows_x, chans), BF16)
    taps = [kernels, taps_other]
    current = None
    saved = []
    for b in range(blocks - 1):
        scratch = [acts_scratch] + weight_scratch
        if b == 0:
            lead, specs = [inputs, lo, hi, inputs_other], [ANY] * 4
            scratch = scratch + [acts_scratch, pltpu.SemaphoreType.DMA((6 * seqs,))]
        else:
            lead, specs = [current], [VMEM]
        got = call(
            functools.partial(forward_kernel, b, b == 0, marks[b]),
            specs + [VMEM, VMEM, ANY, ANY, ANY],
            [sd((seqs, rows_x, chans), BF16)] + [act_shape, slope_shape] * (b + 1),
            scratch,
            8,
        )(*lead, *taps, mixers, near[b], far[b])
        current = got[0]
        saved += [tuple(got[1 + 2 * i : 3 + 2 * i]) for i in range(b + 1)]
        if b == 0:
            current, far[1], cot_other[0], *third = join(current, far[1], cot_other[0], *third)
            if share_bits > 2:
                third.append(flip(third[0], "seq", last_bits[2]))
        else:
            current, *arrived = join(current, *cot_other[1:], *third)
            cot_other[1:], third = arrived[: seqs - 1], arrived[seqs - 1 :]
            near[2] = jnp.concatenate([held[2], *third])
            far[2] = flip(near[2], "seq", 0)

    def both(own, received):
        many = seqs // len(received)

        def plan():
            return [(0, slice(None), 0, ours(0, everything))] + [
                (1 + i, slice(None), 0, theirs(i * many, everything, many)) for i in range(len(received))
            ]

        return pack(plan, 1 + len(received), [own, *received], [sd(inputs.shape, BF16)])[0]

    scale = 1.0 / math.sqrt(all_seqs * bins * n)
    count = n
    size = chans // n
    turned = pltpu.VMEM((count, size, seqs * bins), BF16 if size % 16 == 0 else F32)
    shares = [sd((2, count // 2, size, half), BF16)] * 2

    class Exchange:
        def __init__(self, keep, send, order):
            shape = (2,) * bits + (size, half)
            self.pieces = [keep.reshape(shape), flip(send, "seq", 0).reshape(shape)]
            self.dims = ["ch"] + list(range(bits - 1, 0, -1))
            self.order = list(order)

        def arrived(self, token):
            token, self.pieces[-1] = join(token, self.pieces[-1])
            return token

        def step(self):
            axis = self.order.pop(0)
            at = self.dims.index(axis)
            self.dims.pop(at)
            sent = sum(lax.index_in_dim(p, 1, at, keepdims=False).astype(F32) for p in self.pieces).astype(BF16)
            kept = [lax.index_in_dim(p, 0, at, keepdims=False) for p in self.pieces]
            self.pieces = kept + [flip(sent, "ch", 0) if axis == "ch" else flip(sent, "seq", axis)]
            return sent

        def result(self):
            return sum(p.astype(F32) for p in self.pieces)

    if bits == 4:
        orders = [["ch", 1, 2, 3], [1, 2, "ch", 3], [2, "ch", 1, 3]]
    else:
        orders = [list(range(1, bits)) + ["ch"]] * blocks

    top = blocks - 1
    act, slope = saved[top]
    upper, keep, send = call(
        functools.partial(turn_kernel, scale),
        [VMEM] + [ANY] * 5,
        [slope_shape] + shares,
        [turned, pltpu.SemaphoreType.DMA((6 * seqs,))],
        5,
    )(act, cotangent, lo, hi, *cot_other)
    act, far[2], send = join(act, far[2], send)
    exchanges = [None] * blocks
    exchanges[top] = Exchange(keep, send, orders[top])
    one_shape = sd((1, bins, half), BF16)
    for b in range(top, -1, -1):
        weights = [*taps, mixers, near[b], far[b]]
        slope = saved[b][1]
        scratch = weight_scratch
        if b == top:
            out_own, *out_sent = call(
                functools.partial(output_kernel, b, marks[b]),
                [VMEM, VMEM, ANY, ANY, ANY],
                [seqs_shape] + [one_shape] * seqs,
                weight_scratch,
                4,
            )(current, act, mixers, near[b], far[b])
            out_received = [flip(out_sent[0], "ch", 0)]
            upper, out_own = join(upper, out_own)
            lead, outs = [upper, slope], [slope_shape]
        elif b:
            lead, outs = [upper, slope, saved[b][0]], [slope_shape] + shares
            scratch = scratch + [turned]
        else:
            lead, outs = [upper, slope], [seqs_shape] * 2
        got = call(
            functools.partial(backward_kernel, b, b == top, b == 0, marks[b], scale),
            [VMEM] * (len(lead) + 2) + [ANY, ANY, ANY],
            outs,
            scratch,
            8 if b == top else 6,
        )(*lead, *weights)
        if b == top:
            upper = got[0]
            upper, exchanges[b].pieces[-1], out_received[0] = join(upper, exchanges[b].pieces[-1], out_received[0])
            out_received += [flip(sent, "ch", 0) for sent in out_sent[1:]]
        elif b:
            upper, keep, send = got
            exchanges[b] = Exchange(keep, send, orders[b])
            upper, *out_received[1:] = join(upper, *out_received[1:])
        else:
            in_own, in_sent = got
        if b == 1:
            keep, send = call(
                functools.partial(gradient_kernel, scale),
                [VMEM] * 2,
                shares,
                [turned],
                4,
            )(saved[0][0], upper)
            exchanges[0] = Exchange(keep, send, orders[0])
            arrived = join(upper, *[e.pieces[-1] for e in exchanges])
            upper = arrived[0]
            for e, piece in zip(exchanges, arrived[1:]):
                e.pieces[-1] = piece
                e.step()
    outputs = both(out_own, out_received)
    in_own, outputs, *arrived = join(in_own, outputs, *[e.pieces[-1] for e in exchanges])
    for e, piece in zip(exchanges, arrived):
        e.pieces[-1] = piece
        e.step()
    arrived = join(in_sent, *[e.pieces[-1] for e in exchanges])
    in_sent = arrived[0]
    for e, piece in zip(exchanges, arrived[1:]):
        e.pieces[-1] = piece
    token = fence(token, *[e.step() for e in exchanges], in_sent)
    in_received = flip(in_sent, "ch", 0)
    arrived = join(token, *[e.pieces[-1] for e in exchanges])
    token = arrived[0]
    for e, piece in zip(exchanges, arrived[1:]):
        e.pieces[-1] = piece
        while e.order:
            e.step()
    token, in_received = join(token, in_received)
    grads_token = token
    grads = [e.result() for e in exchanges]
    return outputs, both(in_own, [in_received]), jnp.stack(grads)


def solution(mesh):
    placed = (P(None, "seq", "ch"), P(None, None, "ch"), P(None, None, "ch"), P(None, "seq", "ch"))
    return jax.shard_map(
        on_device,
        mesh=mesh,
        in_specs=placed,
        out_specs=(P(None, "seq", "ch"), P(None, "seq", "ch"), P(None, "seq", "ch")),
        check_vma=False,
    )
```

```python
import functools
import math

import jax
import jax.numpy as jnp
from jax import lax
from jax.experimental import pallas as pl
from jax.experimental.pallas import tpu as pltpu
from jax.sharding import PartitionSpec as P

DILATIONS = (2, 4, 8)
HX = 32
HE = 16
TILE = 256
BF16, F32 = jnp.bfloat16, jnp.float32
VMEM_BYTES = 28 * 1024 * 1024


def flip(value, axis, bit):
    count = lax.axis_size(axis)
    return lax.ppermute(value, axis, [(i, i ^ (1 << bit)) for i in range(count)])


def shift(value, step):
    count = lax.axis_size("seq")
    return lax.ppermute(value, "seq", [(i, i + step) for i in range(count) if 0 <= i + step < count])


def start_all(copies):
    for copy in copies:
        copy.start()


def wait_all(copies):
    for copy in copies:
        copy.wait()


def weight_copies(mix, near, far, weights, sems, block, marks):
    c = lax.axis_index("ch")
    half = mix.shape[1] // 2
    size = near.shape[1]
    per_half = half // size
    parts = 2 * near.shape[0]
    part = lax.axis_index("seq") % parts
    copies = []
    for h in range(2):
        copies.append(
            pltpu.make_async_copy(
                mix.at[block, pl.ds(pl.multiple_of((h ^ c) * half, half), half), :],
                weights.at[0, pl.ds(h * half, half), :],
                sems.at[h],
            )
        )
    for rel in range(parts):
        source = near if rel < parts // 2 else far
        place = part ^ marks[rel]
        row = ((place // per_half) ^ c) * half + (place % per_half) * size
        copies.append(
            pltpu.make_async_copy(
                source.at[rel % (parts // 2)],
                weights.at[1, pl.ds(pl.multiple_of(row, size), size), :],
                sems.at[2 + rel],
            )
        )
    return copies


def gather_copies(own, lo_own, hi_own, partner, buffer, sems, halo, skip):
    c = lax.axis_index("ch")
    seqs = buffer.shape[0]
    bins, half = own.shape[1:]
    low, main, high = pl.ds(0, halo), pl.ds(halo, bins), pl.ds(halo + bins, halo)
    cols = [pl.ds(side * half, half) for side in range(2)]
    pieces = []
    for q in range(seqs):
        at = c * seqs + q
        pieces.append((own.at[at], buffer.at[q, main, cols[0]]))
        pieces.append((lo_own.at[at, pl.ds(skip, halo), :], buffer.at[q, low, cols[0]]))
        pieces.append((hi_own.at[at, pl.ds(skip, halo), :], buffer.at[q, high, cols[0]]))
        other, row = (partner, q) if not isinstance(partner, (list, tuple)) else (partner[q], 0)
        pieces.append((other.at[row, pl.ds(0, bins), :], buffer.at[q, main, cols[1]]))
        pieces.append((other.at[row, pl.ds(bins, halo), :], buffer.at[q, low, cols[1]]))
        pieces.append((other.at[row, pl.ds(bins + halo, halo), :], buffer.at[q, high, cols[1]]))
    return [pltpu.make_async_copy(a, b, sems.at[i]) for i, (a, b) in enumerate(pieces)]


def taps_of(taps, block, tile):
    side, at = divmod(tile * TILE, taps[0].shape[2])
    return [taps[side][block, k : k + 1, at : at + TILE] for k in range(3)]


def activations(block, taps, current, q, tile, keep_rows):
    rows = current.shape[1]
    width = DILATIONS[block]
    cols = slice(tile * TILE, (tile + 1) * TILE)
    k0, k1, k2 = taps_of(taps, block, tile)
    wide = current[q, :, cols].astype(F32)
    pre = k0 * pltpu.roll(wide, width, 0) + k1 * wide + k2 * pltpu.roll(wide, rows - width, 0)
    pre = pre[keep_rows]
    cdf = 0.5 * (1.0 + lax.erf(pre * 0.7071067811865476))
    slope = cdf + pre * jnp.exp(-0.5 * pre * pre) * 0.3989422804014327
    return (pre * cdf).astype(BF16), slope.astype(BF16)


def zero_outside(array, halo):
    seqs, rows, chans = array.shape
    at = lax.axis_index("seq")

    @pl.when(at == 0)
    def _():
        array[:, 0:halo, :] = jnp.zeros((seqs, halo, chans), BF16)

    @pl.when(at == lax.axis_size("seq") - 1)
    def _():
        array[:, rows - halo : rows, :] = jnp.zeros((seqs, halo, chans), BF16)


def mix_tile(acts, weights, tile):
    half = weights.shape[2]
    side, at = divmod(tile * TILE, half)
    return jnp.dot(acts, weights[side, :, at : at + TILE], preferred_element_type=F32)


def forward_kernel(block, first, marks, *refs):
    if first:
        own, lo, hi, partner, t0, t1, mix, near, far, nxt, act_out, slope_out, acts, weights, wsems, current, sems = refs
        loads = gather_copies(own, lo, hi, partner, current, sems, HX, 0)
    else:
        current, t0, t1, mix, near, far, nxt, act_out, slope_out, act_top, slope_top, acts, weights, wsems = refs
        loads = []
    brings = weight_copies(mix, near, far, weights, wsems, block, marks)
    start_all(loads)
    start_all(brings)
    wait_all(loads)
    seqs, rows, chans = current.shape
    bins = rows - 2 * HX
    edge = HX - HE
    for q in range(seqs):
        for tile in range(chans // TILE):
            cols = slice(tile * TILE, (tile + 1) * TILE)
            act, slope = activations(block, (t0, t1), current, q, tile, slice(None))
            slope_out[q, :, cols] = slope[edge : rows - edge]
            acts[q, :, cols] = act
            act_out[q, :, cols] = act[HX : HX + bins]
    wait_all(brings)
    for tile in range(chans // TILE):
        cols = slice(tile * TILE, (tile + 1) * TILE)
        for q in range(seqs):
            nxt[q, :, cols] = (current[q, :, cols].astype(F32) + mix_tile(acts[q], weights, tile)).astype(BF16)
    zero_outside(nxt, HX)
    if not first:
        for q in range(seqs):
            for tile in range(chans // TILE):
                cols = slice(tile * TILE, (tile + 1) * TILE)
                value, slope = activations(block + 1, (t0, t1), nxt, q, tile, slice(edge, rows - edge))
                slope_top[q, :, cols] = slope
                act_top[q, :, cols] = value[HE : HE + bins]


def gradient(act, upper, turned, keep, send, scale, loads=()):
    seqs, bins, chans = act.shape
    half = chans // 2
    c, s = lax.axis_index("ch"), lax.axis_index("seq")
    count, size, _ = turned.shape
    for h in range(2):
        for q in range(seqs):
            flat = act[q, :, h * half : (h + 1) * half].T.astype(turned.dtype)
            for i in range(count // 2):
                rel = ((h ^ c) * (count // 2) + i) ^ s
                place = (rel & 1) * (count // 2) + (rel >> 1)
                turned[place, :, q * bins : (q + 1) * bins] = flat[i * size : (i + 1) * size]
    wait_all(loads)
    for part, target in enumerate((keep, send)):
        first_row = part * (count // 2)
        left = turned[first_row : first_row + count // 2].reshape(count // 2 * size, seqs * bins).astype(BF16)
        for tile in range(chans // TILE):
            cols = slice(tile * TILE, (tile + 1) * TILE)
            side, at = divmod(tile * TILE, half)
            total = sum(
                jnp.dot(left[:, q * bins : (q + 1) * bins], upper[q, HE : HE + bins, cols], preferred_element_type=F32)
                for q in range(seqs)
            )
            total = (total * scale).reshape(count // 2, size, TILE)
            target[side, :, :, at : at + TILE] = total.astype(BF16)


def turn_kernel(scale, act, own, lo, hi, p0, p1, upper, keep, send, turned, sems):
    loads = gather_copies(own, lo, hi, (p0, p1), upper, sems, HE, HX)
    start_all(loads)
    gradient(act, upper, turned, keep, send, scale, loads)


def gradient_kernel(scale, act, upper, keep, send, turned):
    gradient(act, upper, turned, keep, send, scale)


def output_kernel(block, marks, current, act, mix, near, far, out, *refs):
    out_others, weights, wsems = refs[:-2], refs[-2], refs[-1]
    brings = weight_copies(mix, near, far, weights, wsems, block, marks)
    start_all(brings)
    wait_all(brings)
    seqs, bins, chans = act.shape
    half = chans // 2
    for tile in range(chans // TILE):
        cols = slice(tile * TILE, (tile + 1) * TILE)
        side, at = divmod(tile * TILE, half)
        for q in range(seqs):
            value = (current[q, HX : HX + bins, cols].astype(F32) + mix_tile(act[q], weights, tile)).astype(BF16)
            if side:
                out_others[q][0, :, at : at + TILE] = value
            else:
                out[q, :, at : at + TILE] = value


def backward_kernel(block, top, last, marks, scale, *refs):
    if top:
        upper, slopes, t0, t1, mix, near, far, lower, weights, wsems = refs
    elif last:
        upper, slopes, t0, t1, mix, near, far, lower, lower_other, weights, wsems = refs
    else:
        upper, slopes, act, t0, t1, mix, near, far, lower, keep, send, weights, wsems, turned = refs
    brings = weight_copies(mix, near, far, weights, wsems, block, marks)
    start_all(brings)
    if not top and not last:
        gradient(act, upper, turned, keep, send, scale)
    wait_all(brings)
    seqs, rows, chans = upper.shape
    half = chans // 2
    width = DILATIONS[block]
    bins = rows - 2 * HE
    for q in range(seqs):
        for tile in range(chans // TILE):
            cols = slice(tile * TILE, (tile + 1) * TILE)
            side, at = divmod(tile * TILE, half)
            back = sum(
                lax.dot_general(
                    upper[q, :, g * half : (g + 1) * half],
                    weights[g, cols, :],
                    (((1,), (1,)), ((), ())),
                    preferred_element_type=F32,
                )
                for g in range(2)
            )
            slope = (back * slopes[q, :, cols].astype(F32)).astype(BF16).astype(F32)
            k0, k1, k2 = taps_of((t0, t1), block, tile)
            new = upper[q, :, cols].astype(F32) + k0 * pltpu.roll(slope, rows - width, 0) + k1 * slope + k2 * pltpu.roll(slope, width, 0)
            new = new.astype(BF16)
            if last:
                (lower, lower_other)[side][q, :, at : at + TILE] = new[HE : HE + bins]
            else:
                lower[q, :, cols] = new
    if not last:
        zero_outside(lower, HE)


ANY = pl.BlockSpec(memory_space=pl.ANY)
VMEM = pl.BlockSpec(memory_space=pltpu.VMEM)


SHARE = 0.1


def call(kernel, in_specs, outs, scratch, micros, out_specs=None):
    return pl.pallas_call(
        kernel,
        in_specs=in_specs,
        out_specs=out_specs or [VMEM] * len(outs),
        out_shape=outs,
        scratch_shapes=scratch,
        compiler_params=pltpu.CompilerParams(vmem_limit_bytes=VMEM_BYTES),
        cost_estimate=pl.CostEstimate(flops=int(SHARE * micros * 1.15e9), bytes_accessed=int(SHARE * micros * 3.6e6), transcendentals=0),
    )


def pack_kernel(plan, operands, *refs):
    ins, outs, sems = refs[:operands], refs[operands:-1], refs[-1]
    copies = [
        pltpu.make_async_copy(ins[i].at[src], outs[o].at[dst], sems.at[k])
        for k, (i, src, o, dst) in enumerate(plan())
    ]
    start_all(copies)
    wait_all(copies)


def in_hbm(value):
    return pltpu.with_memory_space_constraint(value, pltpu.HBM)


def pack(plan, count, operands, outs):
    return call(
        functools.partial(pack_kernel, plan, len(operands)),
        [ANY] * len(operands),
        outs,
        [pltpu.SemaphoreType.DMA((count,))],
        1,
    )(*operands)


def fence_kernel(token, *refs):
    refs[-1][...] = token[...]


def fence(token, *others):
    return call(
        fence_kernel,
        [VMEM] + [ANY] * len(others),
        [jax.ShapeDtypeStruct(token.shape, token.dtype)],
        [],
        1,
    )(token, *others)[0]


def join(*values):
    return lax.optimization_barrier(values)


def on_device(inputs, kernels, mixers, cotangent):
    all_seqs, bins, half = inputs.shape
    n, m = lax.axis_size("seq"), lax.axis_size("ch")
    seqs, chans = all_seqs // m, half * m
    bits = n.bit_length() - 1
    blocks = mixers.shape[0]
    share_bits = min(3, bits)
    parts = 1 << share_bits
    piece = chans // parts
    sd = jax.ShapeDtypeStruct

    def ours(first, rows):
        return (pl.ds(lax.axis_index("ch") * seqs + first, seqs - first), rows)

    def theirs(first, rows, many=seqs):
        return (pl.ds((1 - lax.axis_index("ch")) * seqs + first, many), rows)

    def mixer_piece(b):
        return (b, pl.ds(pl.multiple_of(lax.axis_index("seq") % parts * piece, piece), piece))

    def third_rows(q):
        size = piece // seqs
        return pl.ds(pl.multiple_of(lax.axis_index("seq") % parts * piece + q * size, size), size)

    everything = pl.ds(0, bins)
    inputs, cotangent, mixers = in_hbm(inputs), in_hbm(cotangent), in_hbm(mixers)

    def first_plan():
        plan = []
        for b in range(2):
            plan.append((2, mixer_piece(b), 0, b))
        for place, (rows_x, rows_e) in enumerate(((pl.ds(bins - HX, HX), pl.ds(bins - HE, HE)), (pl.ds(0, HX), pl.ds(0, HE)))):
            plan.append((0, (slice(None), rows_x), 1 + place, (slice(None), pl.ds(0, HX))))
            plan.append((1, (slice(None), rows_e), 1 + place, (slice(None), pl.ds(HX, HE))))
        return plan

    seqs_shape = sd((seqs, bins, half), BF16)
    halo_shape = sd((all_seqs, HX + HE, half), BF16)
    sent, ups, downs = pack(first_plan, 6, [inputs, cotangent, mixers], [sd((2, piece, half), BF16)] + [halo_shape] * 2)
    fetched = flip(sent, "ch", 0)
    lo, hi = shift(ups, 1), shift(downs, -1)
    taps_other = flip(kernels, "ch", 0)

    def halo_plan(source, halo, skip, out, first, many):
        rows = pl.ds(skip, halo)
        return [
            (source, theirs(first, everything, many), out, (slice(None), everything)),
            (2, theirs(first, rows, many), out, (slice(None), pl.ds(bins, halo))),
            (3, theirs(first, rows, many), out, (slice(None), pl.ds(bins + halo, halo))),
        ]

    sent = pack(
        lambda: [(4, (2, third_rows(q)), 0, (q, pl.ds(bins + 2 * HX, piece // seqs))) for q in range(seqs)]
        + halo_plan(0, HX, 0, 0, 0, seqs)
        + [p for q in range(seqs) for p in halo_plan(1, HE, HX, 1 + q, q, 1)],
        3 + 4 * seqs,
        [inputs, cotangent, lo, hi, mixers],
        [sd((seqs, bins + 2 * HX + piece // seqs, half), BF16)] + [sd((1, bins + 2 * HE, half), BF16)] * seqs,
    )
    inputs_sent, cot_sent = sent[0], sent[1:]

    marks = []
    orders = [list(range(share_bits - 1, 0, -1)) if b % 2 == 0 else list(range(1, share_bits)) for b in range(blocks)]
    for b in range(blocks):
        own_marks = [0]
        for bit in orders[b]:
            own_marks = own_marks + [mark ^ (1 << bit) for mark in own_marks]
        marks.append(tuple(own_marks + [mark ^ 1 for mark in own_marks]))
    last_bits = [order[-1] for order in orders]

    fetched, inputs_sent, taps_other = join(fetched, inputs_sent, taps_other)
    held = [fetched[b : b + 1] for b in range(2)]
    inputs_other = flip(inputs_sent, "ch", 0)
    shared = [[flip(held[b], "seq", bit) for bit in orders[b]] for b in range(2)]
    for b in range(2 if share_bits > 2 else 0):
        shared[b].append(flip(shared[b][0], "seq", last_bits[b]))
    inputs_other, *arrived = join(inputs_other, *shared[0], *shared[1])
    near, far = [None] * blocks, [None] * blocks
    for b in range(2):
        count = len(shared[b])
        near[b] = jnp.concatenate([held[b], *arrived[b * count : (b + 1) * count]])
        far[b] = flip(near[b], "seq", 0)
    held.append(inputs_other[:, bins + 2 * HX :].reshape(1, piece, half))
    third = [flip(held[2], "seq", bit) for bit in orders[2]]
    cot_other = [flip(c, "ch", 0) for c in cot_sent]

    rows_x, rows_e = bins + 2 * HX, bins + 2 * HE
    weight_scratch = [pltpu.VMEM((2, chans, half), BF16), pltpu.SemaphoreType.DMA((2 + parts,))]
    act_shape, slope_shape = sd((seqs, bins, chans), BF16), sd((seqs, rows_e, chans), BF16)
    acts_scratch = pltpu.VMEM((seqs, rows_x, chans), BF16)
    taps = [kernels, taps_other]
    current = None
    saved = []
    for b in range(blocks - 1):
        scratch = [acts_scratch] + weight_scratch
        if b == 0:
            lead, specs = [inputs, lo, hi, inputs_other], [ANY] * 4
            scratch = scratch + [acts_scratch, pltpu.SemaphoreType.DMA((6 * seqs,))]
        else:
            lead, specs = [current], [VMEM]
        got = call(
            functools.partial(forward_kernel, b, b == 0, marks[b]),
            specs + [VMEM, VMEM, ANY, ANY, ANY],
            [sd((seqs, rows_x, chans), BF16)] + [act_shape, slope_shape] * (b + 1),
            scratch,
            8,
        )(*lead, *taps, mixers, near[b], far[b])
        current = got[0]
        saved += [tuple(got[1 + 2 * i : 3 + 2 * i]) for i in range(b + 1)]
        if b == 0:
            current, far[1], cot_other[0], *third = join(current, far[1], cot_other[0], *third)
            if share_bits > 2:
                third.append(flip(third[0], "seq", last_bits[2]))
        else:
            current, *arrived = join(current, *cot_other[1:], *third)
            cot_other[1:], third = arrived[: seqs - 1], arrived[seqs - 1 :]
            near[2] = jnp.concatenate([held[2], *third])
            far[2] = flip(near[2], "seq", 0)

    def both(own, received):
        many = seqs // len(received)

        def plan():
            return [(0, slice(None), 0, ours(0, everything))] + [
                (1 + i, slice(None), 0, theirs(i * many, everything, many)) for i in range(len(received))
            ]

        return pack(plan, 1 + len(received), [own, *received], [sd(inputs.shape, BF16)])[0]

    scale = 1.0 / math.sqrt(all_seqs * bins * n)
    count = n
    size = chans // n
    turned = pltpu.VMEM((count, size, seqs * bins), BF16 if size % 16 == 0 else F32)
    shares = [sd((2, count // 2, size, half), BF16)] * 2

    class Exchange:
        def __init__(self, keep, send, order):
            shape = (2,) * bits + (size, half)
            self.pieces = [keep.reshape(shape), flip(send, "seq", 0).reshape(shape)]
            self.dims = ["ch"] + list(range(bits - 1, 0, -1))
            self.order = list(order)

        def arrived(self, token):
            token, self.pieces[-1] = join(token, self.pieces[-1])
            return token

        def step(self):
            axis = self.order.pop(0)
            at = self.dims.index(axis)
            self.dims.pop(at)
            sent = sum(lax.index_in_dim(p, 1, at, keepdims=False).astype(F32) for p in self.pieces).astype(BF16)
            kept = [lax.index_in_dim(p, 0, at, keepdims=False) for p in self.pieces]
            self.pieces = kept + [flip(sent, "ch", 0) if axis == "ch" else flip(sent, "seq", axis)]
            return sent

        def result(self):
            return sum(p.astype(F32) for p in self.pieces)

    if bits == 4:
        orders = [["ch", 1, 2, 3], [1, 2, "ch", 3], [2, "ch", 1, 3]]
    else:
        orders = [list(range(1, bits)) + ["ch"]] * blocks

    top = blocks - 1
    act, slope = saved[top]
    upper, keep, send = call(
        functools.partial(turn_kernel, scale),
        [VMEM] + [ANY] * 5,
        [slope_shape] + shares,
        [turned, pltpu.SemaphoreType.DMA((6 * seqs,))],
        5,
    )(act, cotangent, lo, hi, *cot_other)
    act, far[2], send = join(act, far[2], send)
    exchanges = [None] * blocks
    exchanges[top] = Exchange(keep, send, orders[top])
    one_shape = sd((1, bins, half), BF16)
    for b in range(top, -1, -1):
        weights = [*taps, mixers, near[b], far[b]]
        slope = saved[b][1]
        scratch = weight_scratch
        if b == top:
            out_own, *out_sent = call(
                functools.partial(output_kernel, b, marks[b]),
                [VMEM, VMEM, ANY, ANY, ANY],
                [seqs_shape] + [one_shape] * seqs,
                weight_scratch,
                4,
            )(current, act, mixers, near[b], far[b])
            out_received = [flip(out_sent[0], "ch", 0)]
            upper, out_own = join(upper, out_own)
            lead, outs = [upper, slope], [slope_shape]
        elif b:
            lead, outs = [upper, slope, saved[b][0]], [slope_shape] + shares
            scratch = scratch + [turned]
        else:
            lead, outs = [upper, slope], [seqs_shape] * 2
        got = call(
            functools.partial(backward_kernel, b, b == top, b == 0, marks[b], scale),
            [VMEM] * (len(lead) + 2) + [ANY, ANY, ANY],
            outs,
            scratch,
            8 if b == top else 6,
        )(*lead, *weights)
        if b == top:
            upper = got[0]
            upper, exchanges[b].pieces[-1], out_received[0] = join(upper, exchanges[b].pieces[-1], out_received[0])
            out_received += [flip(sent, "ch", 0) for sent in out_sent[1:]]
        elif b:
            upper, keep, send = got
            exchanges[b] = Exchange(keep, send, orders[b])
            upper, *out_received[1:] = join(upper, *out_received[1:])
        else:
            in_own, in_sent = got
        if b == 1:
            keep, send = call(
                functools.partial(gradient_kernel, scale),
                [VMEM] * 2,
                shares,
                [turned],
                4,
            )(saved[0][0], upper)
            exchanges[0] = Exchange(keep, send, orders[0])
            for e in exchanges[:0:-1]:
                e.step()
            upper, exchanges[0].pieces[-1] = join(upper, exchanges[0].pieces[-1])
            exchanges[0].step()
    outputs = both(out_own, out_received)
    in_own, outputs, *arrived = join(in_own, outputs, *[e.pieces[-1] for e in exchanges])
    for e, piece in zip(exchanges, arrived):
        e.pieces[-1] = piece
        e.step()
    arrived = join(in_sent, *[e.pieces[-1] for e in exchanges])
    in_sent = arrived[0]
    for e, piece in zip(exchanges, arrived[1:]):
        e.pieces[-1] = piece
    token = fence(fetched[0, :16, :128], *[e.step() for e in exchanges], in_sent)
    in_received = flip(in_sent, "ch", 0)
    arrived = join(token, *[e.pieces[-1] for e in exchanges])
    token = arrived[0]
    for e, piece in zip(exchanges, arrived[1:]):
        e.pieces[-1] = piece
        while e.order:
            e.step()
    token, in_received = join(token, in_received)
    grads_token = token
    grads = [e.result() for e in exchanges]
    return outputs, both(in_own, [in_received]), jnp.stack(grads)


def solution(mesh):
    placed = (P(None, "seq", "ch"), P(None, None, "ch"), P(None, None, "ch"), P(None, "seq", "ch"))
    return jax.shard_map(
        on_device,
        mesh=mesh,
        in_specs=placed,
        out_specs=(P(None, "seq", "ch"), P(None, "seq", "ch"), P(None, "seq", "ch")),
        check_vma=False,
    )
```

```python
import functools
import math

import jax
import jax.numpy as jnp
from jax import lax
from jax.experimental import pallas as pl
from jax.experimental.pallas import tpu as pltpu
from jax.sharding import PartitionSpec as P

DILATIONS = (2, 4, 8)
HX = 32
HE = 16
TILE = 256
BF16, F32 = jnp.bfloat16, jnp.float32
VMEM_BYTES = 28 * 1024 * 1024


def flip(value, axis, bit):
    count = lax.axis_size(axis)
    return lax.ppermute(value, axis, [(i, i ^ (1 << bit)) for i in range(count)])


def shift(value, step):
    count = lax.axis_size("seq")
    return lax.ppermute(value, "seq", [(i, i + step) for i in range(count) if 0 <= i + step < count])


def start_all(copies):
    for copy in copies:
        copy.start()


def wait_all(copies):
    for copy in copies:
        copy.wait()


def weight_copies(mix, near, far, weights, sems, block, marks):
    c = lax.axis_index("ch")
    half = mix.shape[1] // 2
    size = near.shape[1]
    per_half = half // size
    parts = 2 * near.shape[0]
    part = lax.axis_index("seq") % parts
    copies = []
    for h in range(2):
        copies.append(
            pltpu.make_async_copy(
                mix.at[block, pl.ds(pl.multiple_of((h ^ c) * half, half), half), :],
                weights.at[0, pl.ds(h * half, half), :],
                sems.at[h],
            )
        )
    for rel in range(parts):
        source = near if rel < parts // 2 else far
        place = part ^ marks[rel]
        row = ((place // per_half) ^ c) * half + (place % per_half) * size
        copies.append(
            pltpu.make_async_copy(
                source.at[rel % (parts // 2)],
                weights.at[1, pl.ds(pl.multiple_of(row, size), size), :],
                sems.at[2 + rel],
            )
        )
    return copies


def gather_copies(own, lo_own, hi_own, partner, buffer, sems, halo, skip):
    c = lax.axis_index("ch")
    seqs = buffer.shape[0]
    bins, half = own.shape[1:]
    low, main, high = pl.ds(0, halo), pl.ds(halo, bins), pl.ds(halo + bins, halo)
    cols = [pl.ds(side * half, half) for side in range(2)]
    pieces = []
    for q in range(seqs):
        at = c * seqs + q
        pieces.append((own.at[at], buffer.at[q, main, cols[0]]))
        pieces.append((lo_own.at[at, pl.ds(skip, halo), :], buffer.at[q, low, cols[0]]))
        pieces.append((hi_own.at[at, pl.ds(skip, halo), :], buffer.at[q, high, cols[0]]))
        pieces.append((partner.at[q, pl.ds(0, bins), :], buffer.at[q, main, cols[1]]))
        pieces.append((partner.at[q, pl.ds(bins, halo), :], buffer.at[q, low, cols[1]]))
        pieces.append((partner.at[q, pl.ds(bins + halo, halo), :], buffer.at[q, high, cols[1]]))
    return [pltpu.make_async_copy(a, b, sems.at[i]) for i, (a, b) in enumerate(pieces)]


def taps_of(taps, block, tile):
    side, at = divmod(tile * TILE, taps[0].shape[2])
    return [taps[side][block, k : k + 1, at : at + TILE] for k in range(3)]


def activations(block, taps, current, q, tile, keep_rows):
    rows = current.shape[1]
    width = DILATIONS[block]
    cols = slice(tile * TILE, (tile + 1) * TILE)
    k0, k1, k2 = taps_of(taps, block, tile)
    wide = current[q, :, cols].astype(F32)
    pre = k0 * pltpu.roll(wide, width, 0) + k1 * wide + k2 * pltpu.roll(wide, rows - width, 0)
    pre = pre[keep_rows]
    cdf = 0.5 * (1.0 + lax.erf(pre * 0.7071067811865476))
    slope = cdf + pre * jnp.exp(-0.5 * pre * pre) * 0.3989422804014327
    return (pre * cdf).astype(BF16), slope.astype(BF16)


def zero_outside(array, halo):
    seqs, rows, chans = array.shape
    at = lax.axis_index("seq")

    @pl.when(at == 0)
    def _():
        array[:, 0:halo, :] = jnp.zeros((seqs, halo, chans), BF16)

    @pl.when(at == lax.axis_size("seq") - 1)
    def _():
        array[:, rows - halo : rows, :] = jnp.zeros((seqs, halo, chans), BF16)


def mix_tile(acts, weights, tile):
    half = weights.shape[2]
    side, at = divmod(tile * TILE, half)
    return jnp.dot(acts, weights[side, :, at : at + TILE], preferred_element_type=F32)


def forward_kernel(block, first, marks, *refs):
    if first:
        own, lo, hi, partner, t0, t1, mix, near, far, nxt, act_out, slope_out, acts, weights, wsems, current, sems = refs
        loads = gather_copies(own, lo, hi, partner, current, sems, HX, 0)
    else:
        current, t0, t1, mix, near, far, nxt, act_out, slope_out, act_top, slope_top, acts, weights, wsems = refs
        loads = []
    brings = weight_copies(mix, near, far, weights, wsems, block, marks)
    start_all(loads)
    start_all(brings)
    wait_all(loads)
    seqs, rows, chans = current.shape
    bins = rows - 2 * HX
    edge = HX - HE
    for q in range(seqs):
        for tile in range(chans // TILE):
            cols = slice(tile * TILE, (tile + 1) * TILE)
            act, slope = activations(block, (t0, t1), current, q, tile, slice(None))
            slope_out[q, :, cols] = slope[edge : rows - edge]
            acts[q, :, cols] = act
            act_out[q, :, cols] = act[HX : HX + bins]
    wait_all(brings)
    for tile in range(chans // TILE):
        cols = slice(tile * TILE, (tile + 1) * TILE)
        for q in range(seqs):
            nxt[q, :, cols] = (current[q, :, cols].astype(F32) + mix_tile(acts[q], weights, tile)).astype(BF16)
    zero_outside(nxt, HX)
    if not first:
        for q in range(seqs):
            for tile in range(chans // TILE):
                cols = slice(tile * TILE, (tile + 1) * TILE)
                value, slope = activations(block + 1, (t0, t1), nxt, q, tile, slice(edge, rows - edge))
                slope_top[q, :, cols] = slope
                act_top[q, :, cols] = value[HE : HE + bins]


def gradient(act, upper, turned, keep, send, scale, loads=()):
    seqs, bins, chans = act.shape
    half = chans // 2
    c, s = lax.axis_index("ch"), lax.axis_index("seq")
    count, size, _ = turned.shape
    for h in range(2):
        for q in range(seqs):
            flat = act[q, :, h * half : (h + 1) * half].T.astype(turned.dtype)
            for i in range(count // 2):
                rel = ((h ^ c) * (count // 2) + i) ^ s
                place = (rel & 1) * (count // 2) + (rel >> 1)
                turned[place, :, q * bins : (q + 1) * bins] = flat[i * size : (i + 1) * size]
    wait_all(loads)
    for part, target in enumerate((keep, send)):
        first_row = part * (count // 2)
        left = turned[first_row : first_row + count // 2].reshape(count // 2 * size, seqs * bins).astype(BF16)
        for tile in range(chans // TILE):
            cols = slice(tile * TILE, (tile + 1) * TILE)
            side, at = divmod(tile * TILE, half)
            total = sum(
                jnp.dot(left[:, q * bins : (q + 1) * bins], upper[q, HE : HE + bins, cols], preferred_element_type=F32)
                for q in range(seqs)
            )
            total = (total * scale).reshape(count // 2, size, TILE)
            target[side, :, :, at : at + TILE] = total.astype(BF16)


def turn_kernel(scale, act, own, lo, hi, partner, upper, keep, send, turned, sems):
    loads = gather_copies(own, lo, hi, partner, upper, sems, HE, HX)
    start_all(loads)
    gradient(act, upper, turned, keep, send, scale, loads)


def gradient_kernel(scale, act, upper, keep, send, turned):
    gradient(act, upper, turned, keep, send, scale)


def output_kernel(block, marks, current, act, mix, near, far, out, out_other, weights, wsems):
    brings = weight_copies(mix, near, far, weights, wsems, block, marks)
    start_all(brings)
    wait_all(brings)
    seqs, bins, chans = act.shape
    half = chans // 2
    for tile in range(chans // TILE):
        cols = slice(tile * TILE, (tile + 1) * TILE)
        side, at = divmod(tile * TILE, half)
        for q in range(seqs):
            value = (current[q, HX : HX + bins, cols].astype(F32) + mix_tile(act[q], weights, tile)).astype(BF16)
            (out, out_other)[side][q, :, at : at + TILE] = value


def backward_kernel(block, top, last, marks, scale, *refs):
    if top:
        upper, slopes, t0, t1, mix, near, far, lower, weights, wsems = refs
    elif last:
        upper, slopes, t0, t1, mix, near, far, lower, lower_other, weights, wsems = refs
    else:
        upper, slopes, act, t0, t1, mix, near, far, lower, keep, send, weights, wsems, turned = refs
    brings = weight_copies(mix, near, far, weights, wsems, block, marks)
    start_all(brings)
    if not top and not last:
        gradient(act, upper, turned, keep, send, scale)
    wait_all(brings)
    seqs, rows, chans = upper.shape
    half = chans // 2
    width = DILATIONS[block]
    bins = rows - 2 * HE
    for q in range(seqs):
        for tile in range(chans // TILE):
            cols = slice(tile * TILE, (tile + 1) * TILE)
            side, at = divmod(tile * TILE, half)
            back = sum(
                lax.dot_general(
                    upper[q, :, g * half : (g + 1) * half],
                    weights[g, cols, :],
                    (((1,), (1,)), ((), ())),
                    preferred_element_type=F32,
                )
                for g in range(2)
            )
            slope = (back * slopes[q, :, cols].astype(F32)).astype(BF16).astype(F32)
            k0, k1, k2 = taps_of((t0, t1), block, tile)
            new = upper[q, :, cols].astype(F32) + k0 * pltpu.roll(slope, rows - width, 0) + k1 * slope + k2 * pltpu.roll(slope, width, 0)
            new = new.astype(BF16)
            if last:
                (lower, lower_other)[side][q, :, at : at + TILE] = new[HE : HE + bins]
            else:
                lower[q, :, cols] = new
    if not last:
        zero_outside(lower, HE)


ANY = pl.BlockSpec(memory_space=pl.ANY)
VMEM = pl.BlockSpec(memory_space=pltpu.VMEM)


SHARE = 0.1


def call(kernel, in_specs, outs, scratch, micros, out_specs=None):
    return pl.pallas_call(
        kernel,
        in_specs=in_specs,
        out_specs=out_specs or [VMEM] * len(outs),
        out_shape=outs,
        scratch_shapes=scratch,
        compiler_params=pltpu.CompilerParams(vmem_limit_bytes=VMEM_BYTES),
        cost_estimate=pl.CostEstimate(flops=int(SHARE * micros * 1.15e9), bytes_accessed=int(SHARE * micros * 3.6e6), transcendentals=0),
    )


def pack_kernel(plan, operands, *refs):
    ins, outs, sems = refs[:operands], refs[operands:-1], refs[-1]
    copies = [
        pltpu.make_async_copy(ins[i].at[src], outs[o].at[dst], sems.at[k])
        for k, (i, src, o, dst) in enumerate(plan())
    ]
    start_all(copies)
    wait_all(copies)


def in_hbm(value):
    return pltpu.with_memory_space_constraint(value, pltpu.HBM)


def pack(plan, count, operands, outs):
    return call(
        functools.partial(pack_kernel, plan, len(operands)),
        [ANY] * len(operands),
        outs,
        [pltpu.SemaphoreType.DMA((count,))],
        1,
    )(*operands)


def fence_kernel(token, *refs):
    refs[-1][...] = token[...]


def fence(token, *others):
    return call(
        fence_kernel,
        [VMEM] + [ANY] * len(others),
        [jax.ShapeDtypeStruct(token.shape, token.dtype)],
        [],
        1,
    )(token, *others)[0]


def join(*values):
    return lax.optimization_barrier(values)


def on_device(inputs, kernels, mixers, cotangent):
    all_seqs, bins, half = inputs.shape
    n, m = lax.axis_size("seq"), lax.axis_size("ch")
    seqs, chans = all_seqs // m, half * m
    bits = n.bit_length() - 1
    blocks = mixers.shape[0]
    share_bits = min(3, bits)
    parts = 1 << share_bits
    piece = chans // parts
    sd = jax.ShapeDtypeStruct

    def ours(first, rows):
        return (pl.ds(lax.axis_index("ch") * seqs + first, seqs - first), rows)

    def theirs(first, rows, many=seqs):
        return (pl.ds((1 - lax.axis_index("ch")) * seqs + first, many), rows)

    def mixer_piece(b):
        return (b, pl.ds(pl.multiple_of(lax.axis_index("seq") % parts * piece, piece), piece))

    def third_rows(q):
        size = piece // seqs
        return pl.ds(pl.multiple_of(lax.axis_index("seq") % parts * piece + q * size, size), size)

    everything = pl.ds(0, bins)
    inputs, cotangent, mixers = in_hbm(inputs), in_hbm(cotangent), in_hbm(mixers)

    def first_plan():
        plan = []
        for b in range(2):
            plan.append((2, mixer_piece(b), 0, b))
        for place, (rows_x, rows_e) in enumerate(((pl.ds(bins - HX, HX), pl.ds(bins - HE, HE)), (pl.ds(0, HX), pl.ds(0, HE)))):
            plan.append((0, (slice(None), rows_x), 1 + place, (slice(None), pl.ds(0, HX))))
            plan.append((1, (slice(None), rows_e), 1 + place, (slice(None), pl.ds(HX, HE))))
        return plan

    seqs_shape = sd((seqs, bins, half), BF16)
    halo_shape = sd((all_seqs, HX + HE, half), BF16)
    sent, ups, downs = pack(first_plan, 6, [inputs, cotangent, mixers], [sd((2, piece, half), BF16)] + [halo_shape] * 2)
    fetched = flip(sent, "ch", 0)
    lo, hi = shift(ups, 1), shift(downs, -1)
    taps_other = flip(kernels, "ch", 0)

    def halo_plan(source, halo, skip, out, first, many):
        rows = pl.ds(skip, halo)
        return [
            (source, theirs(first, everything, many), out, (slice(None), everything)),
            (2, theirs(first, rows, many), out, (slice(None), pl.ds(bins, halo))),
            (3, theirs(first, rows, many), out, (slice(None), pl.ds(bins + halo, halo))),
        ]

    sent = pack(
        lambda: [(4, (2, third_rows(q)), 0, (q, pl.ds(bins + 2 * HX, piece // seqs))) for q in range(seqs)]
        + halo_plan(0, HX, 0, 0, 0, seqs)
        + halo_plan(1, HE, HX, 1, 0, seqs),
        6 + seqs,
        [inputs, cotangent, lo, hi, mixers],
        [sd((seqs, bins + 2 * HX + piece // seqs, half), BF16), sd((seqs, bins + 2 * HE, half), BF16)],
    )
    inputs_sent, cot_sent = sent

    marks = []
    orders = [list(range(share_bits - 1, 0, -1)) if b % 2 == 0 else list(range(1, share_bits)) for b in range(blocks)]
    for b in range(blocks):
        own_marks = [0]
        for bit in orders[b]:
            own_marks = own_marks + [mark ^ (1 << bit) for mark in own_marks]
        marks.append(tuple(own_marks + [mark ^ 1 for mark in own_marks]))
    last_bits = [order[-1] for order in orders]

    fetched, inputs_sent, taps_other = join(fetched, inputs_sent, taps_other)
    held = [fetched[b : b + 1] for b in range(2)]
    inputs_other = flip(inputs_sent, "ch", 0)
    shared = [[flip(held[b], "seq", bit) for bit in orders[b]] for b in range(2)]
    for b in range(2 if share_bits > 2 else 0):
        shared[b].append(flip(shared[b][0], "seq", last_bits[b]))
    inputs_other, *arrived = join(inputs_other, *shared[0], *shared[1])
    near, far = [None] * blocks, [None] * blocks
    for b in range(2):
        count = len(shared[b])
        near[b] = jnp.concatenate([held[b], *arrived[b * count : (b + 1) * count]])
        far[b] = flip(near[b], "seq", 0)
    held.append(inputs_other[:, bins + 2 * HX :].reshape(1, piece, half))
    third = [flip(held[2], "seq", bit) for bit in orders[2]]
    cot_other = flip(cot_sent, "ch", 0)

    rows_x, rows_e = bins + 2 * HX, bins + 2 * HE
    weight_scratch = [pltpu.VMEM((2, chans, half), BF16), pltpu.SemaphoreType.DMA((2 + parts,))]
    act_shape, slope_shape = sd((seqs, bins, chans), BF16), sd((seqs, rows_e, chans), BF16)
    acts_scratch = pltpu.VMEM((seqs, rows_x, chans), BF16)
    taps = [kernels, taps_other]
    current = None
    saved = []
    for b in range(blocks - 1):
        scratch = [acts_scratch] + weight_scratch
        if b == 0:
            lead, specs = [inputs, lo, hi, inputs_other], [ANY] * 4
            scratch = scratch + [acts_scratch, pltpu.SemaphoreType.DMA((6 * seqs,))]
        else:
            lead, specs = [current], [VMEM]
        got = call(
            functools.partial(forward_kernel, b, b == 0, marks[b]),
            specs + [VMEM, VMEM, ANY, ANY, ANY],
            [sd((seqs, rows_x, chans), BF16)] + [act_shape, slope_shape] * (b + 1),
            scratch,
            8,
        )(*lead, *taps, mixers, near[b], far[b])
        current = got[0]
        saved += [tuple(got[1 + 2 * i : 3 + 2 * i]) for i in range(b + 1)]
        if b == 0:
            current, far[1], *third = join(current, far[1], *third)
            if share_bits > 2:
                third.append(flip(third[0], "seq", last_bits[2]))
        else:
            current, cot_other, *third = join(current, cot_other, *third)
            near[2] = jnp.concatenate([held[2], *third])
            far[2] = flip(near[2], "seq", 0)

    def both(own, received):
        many = seqs // len(received)

        def plan():
            return [(0, slice(None), 0, ours(0, everything))] + [
                (1 + i, slice(None), 0, theirs(i * many, everything, many)) for i in range(len(received))
            ]

        return pack(plan, 1 + len(received), [own, *received], [sd(inputs.shape, BF16)])[0]

    scale = 1.0 / math.sqrt(all_seqs * bins * n)
    count = n
    size = chans // n
    turned = pltpu.VMEM((count, size, seqs * bins), BF16 if size % 16 == 0 else F32)
    shares = [sd((2, count // 2, size, half), BF16)] * 2

    class Exchange:
        def __init__(self, keep, send, order):
            shape = (2,) * bits + (size, half)
            self.pieces = [keep.reshape(shape), flip(send, "seq", 0).reshape(shape)]
            self.dims = ["ch"] + list(range(bits - 1, 0, -1))
            self.order = list(order)

        def arrived(self, token):
            token, self.pieces[-1] = join(token, self.pieces[-1])
            return token

        def step(self):
            axis = self.order.pop(0)
            at = self.dims.index(axis)
            self.dims.pop(at)
            sent = sum(lax.index_in_dim(p, 1, at, keepdims=False).astype(F32) for p in self.pieces).astype(BF16)
            kept = [lax.index_in_dim(p, 0, at, keepdims=False) for p in self.pieces]
            self.pieces = kept + [flip(sent, "ch", 0) if axis == "ch" else flip(sent, "seq", axis)]
            return sent

        def result(self):
            return sum(p.astype(F32) for p in self.pieces)

    if bits == 4:
        orders = [["ch", 1, 2, 3], [1, 2, "ch", 3], [2, "ch", 1, 3]]
    else:
        orders = [list(range(1, bits)) + ["ch"]] * blocks

    top = blocks - 1
    act, slope = saved[top]
    upper, keep, send = call(
        functools.partial(turn_kernel, scale),
        [VMEM] + [ANY] * 4,
        [slope_shape] + shares,
        [turned, pltpu.SemaphoreType.DMA((6 * seqs,))],
        5,
    )(act, cotangent, lo, hi, cot_other)
    act, far[2], send = join(act, far[2], send)
    exchanges = [None] * blocks
    exchanges[top] = Exchange(keep, send, orders[top])
    for b in range(top, -1, -1):
        weights = [*taps, mixers, near[b], far[b]]
        slope = saved[b][1]
        scratch = weight_scratch
        if b == top:
            out_own, out_sent = call(
                functools.partial(output_kernel, b, marks[b]),
                [VMEM, VMEM, ANY, ANY, ANY],
                [seqs_shape] * 2,
                weight_scratch,
                4,
            )(current, act, mixers, near[b], far[b])
            out_received = [flip(out_sent, "ch", 0)]
            upper, out_own = join(upper, out_own)
            lead, outs = [upper, slope], [slope_shape]
        elif b:
            lead, outs = [upper, slope, saved[b][0]], [slope_shape] + shares
            scratch = scratch + [turned]
        else:
            lead, outs = [upper, slope], [seqs_shape] * 2
        got = call(
            functools.partial(backward_kernel, b, b == top, b == 0, marks[b], scale),
            [VMEM] * (len(lead) + 2) + [ANY, ANY, ANY],
            outs,
            scratch,
            8 if b == top else 6,
        )(*lead, *weights)
        if b == top:
            upper = got[0]
            upper, exchanges[b].pieces[-1] = join(upper, exchanges[b].pieces[-1])
        elif b:
            upper, keep, send = got
            exchanges[b] = Exchange(keep, send, orders[b])
            upper, out_received[0] = join(upper, out_received[0])
        else:
            in_own, in_sent = got
        if b == 1:
            keep, send = call(
                functools.partial(gradient_kernel, scale),
                [VMEM] * 2,
                shares,
                [turned],
                4,
            )(saved[0][0], upper)
            exchanges[0] = Exchange(keep, send, orders[0])
            for e in exchanges[:0:-1]:
                e.step()
            upper, exchanges[0].pieces[-1] = join(upper, exchanges[0].pieces[-1])
            exchanges[0].step()
    outputs = both(out_own, out_received)
    in_own, outputs, *arrived = join(in_own, outputs, *[e.pieces[-1] for e in exchanges])
    for e, piece in zip(exchanges, arrived):
        e.pieces[-1] = piece
        e.step()
    arrived = join(in_sent, *[e.pieces[-1] for e in exchanges])
    in_sent = arrived[0]
    for e, piece in zip(exchanges, arrived[1:]):
        e.pieces[-1] = piece
    token = fence(fetched[0, :16, :128], *[e.step() for e in exchanges], in_sent)
    in_received = flip(in_sent, "ch", 0)
    arrived = join(token, *[e.pieces[-1] for e in exchanges])
    token = arrived[0]
    for e, piece in zip(exchanges, arrived[1:]):
        e.pieces[-1] = piece
        while e.order:
            e.step()
    arrived = join(both(in_own, [in_received]), *[e.pieces[-1] for e in exchanges])
    input_grad = arrived[0]
    for e, piece in zip(exchanges, arrived[1:]):
        e.pieces[-1] = piece
    grads_token = token
    grads = [e.result() for e in exchanges]
    return outputs, input_grad, jnp.stack(grads)


def solution(mesh):
    placed = (P(None, "seq", "ch"), P(None, None, "ch"), P(None, None, "ch"), P(None, "seq", "ch"))
    return jax.shard_map(
        on_device,
        mesh=mesh,
        in_specs=placed,
        out_specs=(P(None, "seq", "ch"), P(None, "seq", "ch"), P(None, "seq", "ch")),
        check_vma=False,
    )
```

```python
import functools
import math

import jax
import jax.numpy as jnp
from jax import lax
from jax.experimental import pallas as pl
from jax.experimental.pallas import tpu as pltpu
from jax.sharding import PartitionSpec as P

DILATIONS = (2, 4, 8)
HX = 32
HE = 16
TILE = 256
BF16, F32 = jnp.bfloat16, jnp.float32
VMEM_BYTES = 28 * 1024 * 1024


def flip(value, axis, bit):
    count = lax.axis_size(axis)
    return lax.ppermute(value, axis, [(i, i ^ (1 << bit)) for i in range(count)])


def shift(value, step):
    count = lax.axis_size("seq")
    return lax.ppermute(value, "seq", [(i, i + step) for i in range(count) if 0 <= i + step < count])


def start_all(copies):
    for copy in copies:
        copy.start()


def wait_all(copies):
    for copy in copies:
        copy.wait()


def weight_copies(mix, near, far, weights, sems, block, marks):
    c = lax.axis_index("ch")
    half = mix.shape[1] // 2
    size = near.shape[1]
    per_half = half // size
    parts = 2 * near.shape[0]
    part = lax.axis_index("seq") % parts
    copies = []
    for h in range(2):
        copies.append(
            pltpu.make_async_copy(
                mix.at[block, pl.ds(pl.multiple_of((h ^ c) * half, half), half), :],
                weights.at[0, pl.ds(h * half, half), :],
                sems.at[h],
            )
        )
    for rel in range(parts):
        source = near if rel < parts // 2 else far
        place = part ^ marks[rel]
        row = ((place // per_half) ^ c) * half + (place % per_half) * size
        copies.append(
            pltpu.make_async_copy(
                source.at[rel % (parts // 2)],
                weights.at[1, pl.ds(pl.multiple_of(row, size), size), :],
                sems.at[2 + rel],
            )
        )
    return copies


def gather_copies(own, lo_own, hi_own, partner, buffer, sems, halo, skip):
    c = lax.axis_index("ch")
    seqs = buffer.shape[0]
    bins, half = own.shape[1:]
    low, main, high = pl.ds(0, halo), pl.ds(halo, bins), pl.ds(halo + bins, halo)
    cols = [pl.ds(side * half, half) for side in range(2)]
    pieces = []
    for q in range(seqs):
        at = c * seqs + q
        pieces.append((own.at[at], buffer.at[q, main, cols[0]]))
        pieces.append((lo_own.at[at, pl.ds(skip, halo), :], buffer.at[q, low, cols[0]]))
        pieces.append((hi_own.at[at, pl.ds(skip, halo), :], buffer.at[q, high, cols[0]]))
        pieces.append((partner.at[q, pl.ds(0, bins), :], buffer.at[q, main, cols[1]]))
        pieces.append((partner.at[q, pl.ds(bins, halo), :], buffer.at[q, low, cols[1]]))
        pieces.append((partner.at[q, pl.ds(bins + halo, halo), :], buffer.at[q, high, cols[1]]))
    return [pltpu.make_async_copy(a, b, sems.at[i]) for i, (a, b) in enumerate(pieces)]


def taps_of(taps, block, tile):
    side, at = divmod(tile * TILE, taps[0].shape[2])
    return [taps[side][block, k : k + 1, at : at + TILE] for k in range(3)]


def activations(block, taps, current, q, tile, keep_rows):
    rows = current.shape[1]
    width = DILATIONS[block]
    cols = slice(tile * TILE, (tile + 1) * TILE)
    k0, k1, k2 = taps_of(taps, block, tile)
    wide = current[q, :, cols].astype(F32)
    pre = k0 * pltpu.roll(wide, width, 0) + k1 * wide + k2 * pltpu.roll(wide, rows - width, 0)
    pre = pre[keep_rows]
    cdf = 0.5 * (1.0 + lax.erf(pre * 0.7071067811865476))
    slope = cdf + pre * jnp.exp(-0.5 * pre * pre) * 0.3989422804014327
    return (pre * cdf).astype(BF16), slope.astype(BF16)


def zero_outside(array, halo):
    seqs, rows, chans = array.shape
    at = lax.axis_index("seq")

    @pl.when(at == 0)
    def _():
        array[:, 0:halo, :] = jnp.zeros((seqs, halo, chans), BF16)

    @pl.when(at == lax.axis_size("seq") - 1)
    def _():
        array[:, rows - halo : rows, :] = jnp.zeros((seqs, halo, chans), BF16)


def mix_tile(acts, weights, tile):
    half = weights.shape[2]
    side, at = divmod(tile * TILE, half)
    return jnp.dot(acts, weights[side, :, at : at + TILE], preferred_element_type=F32)


def forward_kernel(block, first, marks, *refs):
    if first:
        own, lo, hi, partner, t0, t1, mix, near, far, nxt, act_out, slope_out, acts, weights, wsems, current, sems = refs
        loads = gather_copies(own, lo, hi, partner, current, sems, HX, 0)
    else:
        current, t0, t1, mix, near, far, nxt, act_out, slope_out, act_top, slope_top, acts, weights, wsems = refs
        loads = []
    brings = weight_copies(mix, near, far, weights, wsems, block, marks)
    start_all(loads)
    start_all(brings)
    wait_all(loads)
    seqs, rows, chans = current.shape
    bins = rows - 2 * HX
    edge = HX - HE
    for q in range(seqs):
        for tile in range(chans // TILE):
            cols = slice(tile * TILE, (tile + 1) * TILE)
            act, slope = activations(block, (t0, t1), current, q, tile, slice(None))
            slope_out[q, :, cols] = slope[edge : rows - edge]
            acts[q, :, cols] = act
            act_out[q, :, cols] = act[HX : HX + bins]
    wait_all(brings)
    for tile in range(chans // TILE):
        cols = slice(tile * TILE, (tile + 1) * TILE)
        for q in range(seqs):
            nxt[q, :, cols] = (current[q, :, cols].astype(F32) + mix_tile(acts[q], weights, tile)).astype(BF16)
    zero_outside(nxt, HX)
    if not first:
        for q in range(seqs):
            for tile in range(chans // TILE):
                cols = slice(tile * TILE, (tile + 1) * TILE)
                value, slope = activations(block + 1, (t0, t1), nxt, q, tile, slice(edge, rows - edge))
                slope_top[q, :, cols] = slope
                act_top[q, :, cols] = value[HE : HE + bins]


def gradient(act, upper, turned, keep, send, scale, loads=()):
    seqs, bins, chans = act.shape
    half = chans // 2
    c, s = lax.axis_index("ch"), lax.axis_index("seq")
    count, size, _ = turned.shape
    for h in range(2):
        for q in range(seqs):
            flat = act[q, :, h * half : (h + 1) * half].T.astype(turned.dtype)
            for i in range(count // 2):
                rel = ((h ^ c) * (count // 2) + i) ^ s
                place = (rel & 1) * (count // 2) + (rel >> 1)
                turned[place, :, q * bins : (q + 1) * bins] = flat[i * size : (i + 1) * size]
    wait_all(loads)
    for part, target in enumerate((keep, send)):
        first_row = part * (count // 2)
        left = turned[first_row : first_row + count // 2].reshape(count // 2 * size, seqs * bins).astype(BF16)
        for tile in range(chans // TILE):
            cols = slice(tile * TILE, (tile + 1) * TILE)
            side, at = divmod(tile * TILE, half)
            total = sum(
                jnp.dot(left[:, q * bins : (q + 1) * bins], upper[q, HE : HE + bins, cols], preferred_element_type=F32)
                for q in range(seqs)
            )
            total = (total * scale).reshape(count // 2, size, TILE)
            target[side, :, :, at : at + TILE] = total.astype(BF16)


def turn_kernel(scale, act, own, lo, hi, partner, upper, keep, send, turned, sems):
    loads = gather_copies(own, lo, hi, partner, upper, sems, HE, HX)
    start_all(loads)
    gradient(act, upper, turned, keep, send, scale, loads)


def gradient_kernel(scale, act, upper, keep, send, turned):
    gradient(act, upper, turned, keep, send, scale)


def output_kernel(block, marks, current, act, mix, near, far, out, out_other, weights, wsems):
    brings = weight_copies(mix, near, far, weights, wsems, block, marks)
    start_all(brings)
    wait_all(brings)
    seqs, bins, chans = act.shape
    half = chans // 2
    for tile in range(chans // TILE):
        cols = slice(tile * TILE, (tile + 1) * TILE)
        side, at = divmod(tile * TILE, half)
        for q in range(seqs):
            value = (current[q, HX : HX + bins, cols].astype(F32) + mix_tile(act[q], weights, tile)).astype(BF16)
            (out, out_other)[side][q, :, at : at + TILE] = value


def backward_kernel(block, top, last, marks, scale, *refs):
    if top:
        upper, slopes, t0, t1, mix, near, far, lower, weights, wsems = refs
    elif last:
        upper, slopes, t0, t1, mix, near, far, lower, lower_other, weights, wsems = refs
    else:
        upper, slopes, act, t0, t1, mix, near, far, lower, keep, send, weights, wsems, turned = refs
    brings = weight_copies(mix, near, far, weights, wsems, block, marks)
    start_all(brings)
    if not top and not last:
        gradient(act, upper, turned, keep, send, scale)
    wait_all(brings)
    seqs, rows, chans = upper.shape
    half = chans // 2
    width = DILATIONS[block]
    bins = rows - 2 * HE
    for q in range(seqs):
        for tile in range(chans // TILE):
            cols = slice(tile * TILE, (tile + 1) * TILE)
            side, at = divmod(tile * TILE, half)
            back = sum(
                lax.dot_general(
                    upper[q, :, g * half : (g + 1) * half],
                    weights[g, cols, :],
                    (((1,), (1,)), ((), ())),
                    preferred_element_type=F32,
                )
                for g in range(2)
            )
            slope = (back * slopes[q, :, cols].astype(F32)).astype(BF16).astype(F32)
            k0, k1, k2 = taps_of((t0, t1), block, tile)
            new = upper[q, :, cols].astype(F32) + k0 * pltpu.roll(slope, rows - width, 0) + k1 * slope + k2 * pltpu.roll(slope, width, 0)
            new = new.astype(BF16)
            if last:
                (lower, lower_other)[side][q, :, at : at + TILE] = new[HE : HE + bins]
            else:
                lower[q, :, cols] = new
    if not last:
        zero_outside(lower, HE)


ANY = pl.BlockSpec(memory_space=pl.ANY)
VMEM = pl.BlockSpec(memory_space=pltpu.VMEM)


SHARE = 0.05


def call(kernel, in_specs, outs, scratch, micros, out_specs=None):
    return pl.pallas_call(
        kernel,
        in_specs=in_specs,
        out_specs=out_specs or [VMEM] * len(outs),
        out_shape=outs,
        scratch_shapes=scratch,
        compiler_params=pltpu.CompilerParams(vmem_limit_bytes=VMEM_BYTES),
        cost_estimate=pl.CostEstimate(flops=int(SHARE * micros * 1.15e9), bytes_accessed=int(SHARE * micros * 3.6e6), transcendentals=0),
    )


def pack_kernel(plan, operands, *refs):
    ins, outs, sems = refs[:operands], refs[operands:-1], refs[-1]
    copies = [
        pltpu.make_async_copy(ins[i].at[src], outs[o].at[dst], sems.at[k])
        for k, (i, src, o, dst) in enumerate(plan())
    ]
    start_all(copies)
    wait_all(copies)


def in_hbm(value):
    return pltpu.with_memory_space_constraint(value, pltpu.HBM)


def pack(plan, count, operands, outs):
    return call(
        functools.partial(pack_kernel, plan, len(operands)),
        [ANY] * len(operands),
        outs,
        [pltpu.SemaphoreType.DMA((count,))],
        1,
    )(*operands)


def fence_kernel(token, *refs):
    refs[-1][...] = token[...]


def fence(token, *others):
    return call(
        fence_kernel,
        [VMEM] + [ANY] * len(others),
        [jax.ShapeDtypeStruct(token.shape, token.dtype)],
        [],
        1,
    )(token, *others)[0]


def join(*values):
    return lax.optimization_barrier(values)


def on_device(inputs, kernels, mixers, cotangent):
    all_seqs, bins, half = inputs.shape
    n, m = lax.axis_size("seq"), lax.axis_size("ch")
    seqs, chans = all_seqs // m, half * m
    bits = n.bit_length() - 1
    blocks = mixers.shape[0]
    share_bits = min(3, bits)
    parts = 1 << share_bits
    piece = chans // parts
    sd = jax.ShapeDtypeStruct

    def ours(first, rows):
        return (pl.ds(lax.axis_index("ch") * seqs + first, seqs - first), rows)

    def theirs(first, rows, many=seqs):
        return (pl.ds((1 - lax.axis_index("ch")) * seqs + first, many), rows)

    def mixer_piece(b):
        return (b, pl.ds(pl.multiple_of(lax.axis_index("seq") % parts * piece, piece), piece))

    def third_rows(q):
        size = piece // seqs
        return pl.ds(pl.multiple_of(lax.axis_index("seq") % parts * piece + q * size, size), size)

    everything = pl.ds(0, bins)
    inputs, cotangent, mixers = in_hbm(inputs), in_hbm(cotangent), in_hbm(mixers)

    def first_plan():
        plan = []
        for b in range(2):
            plan.append((2, mixer_piece(b), 0, b))
        for place, (rows_x, rows_e) in enumerate(((pl.ds(bins - HX, HX), pl.ds(bins - HE, HE)), (pl.ds(0, HX), pl.ds(0, HE)))):
            plan.append((0, (slice(None), rows_x), 1 + place, (slice(None), pl.ds(0, HX))))
            plan.append((1, (slice(None), rows_e), 1 + place, (slice(None), pl.ds(HX, HE))))
        return plan

    seqs_shape = sd((seqs, bins, half), BF16)
    halo_shape = sd((all_seqs, HX + HE, half), BF16)
    sent, ups, downs = pack(first_plan, 6, [inputs, cotangent, mixers], [sd((2, piece, half), BF16)] + [halo_shape] * 2)
    fetched = flip(sent, "ch", 0)
    lo, hi = shift(ups, 1), shift(downs, -1)
    taps_other = flip(kernels, "ch", 0)

    def halo_plan(source, halo, skip, out, first, many):
        rows = pl.ds(skip, halo)
        return [
            (source, theirs(first, everything, many), out, (slice(None), everything)),
            (2, theirs(first, rows, many), out, (slice(None), pl.ds(bins, halo))),
            (3, theirs(first, rows, many), out, (slice(None), pl.ds(bins + halo, halo))),
        ]

    sent = pack(
        lambda: [(4, (2, third_rows(q)), 0, (q, pl.ds(bins + 2 * HX, piece // seqs))) for q in range(seqs)]
        + halo_plan(0, HX, 0, 0, 0, seqs)
        + halo_plan(1, HE, HX, 1, 0, seqs),
        6 + seqs,
        [inputs, cotangent, lo, hi, mixers],
        [sd((seqs, bins + 2 * HX + piece // seqs, half), BF16), sd((seqs, bins + 2 * HE, half), BF16)],
    )
    inputs_sent, cot_sent = sent

    marks = []
    orders = [list(range(share_bits - 1, 0, -1)) if b % 2 == 0 else list(range(1, share_bits)) for b in range(blocks)]
    for b in range(blocks):
        own_marks = [0]
        for bit in orders[b]:
            own_marks = own_marks + [mark ^ (1 << bit) for mark in own_marks]
        marks.append(tuple(own_marks + [mark ^ 1 for mark in own_marks]))
    last_bits = [order[-1] for order in orders]

    fetched, inputs_sent, taps_other = join(fetched, inputs_sent, taps_other)
    held = [fetched[b : b + 1] for b in range(2)]
    inputs_other = flip(inputs_sent, "ch", 0)
    shared = [[flip(held[b], "seq", bit) for bit in orders[b]] for b in range(2)]
    for b in range(2 if share_bits > 2 else 0):
        shared[b].append(flip(shared[b][0], "seq", last_bits[b]))
    inputs_other, *arrived = join(inputs_other, *shared[0], *shared[1])
    near, far = [None] * blocks, [None] * blocks
    for b in range(2):
        count = len(shared[b])
        near[b] = jnp.concatenate([held[b], *arrived[b * count : (b + 1) * count]])
        far[b] = flip(near[b], "seq", 0)
    held.append(inputs_other[:, bins + 2 * HX :].reshape(1, piece, half))
    third = [flip(held[2], "seq", bit) for bit in orders[2]]
    cot_other = flip(cot_sent, "ch", 0)

    rows_x, rows_e = bins + 2 * HX, bins + 2 * HE
    weight_scratch = [pltpu.VMEM((2, chans, half), BF16), pltpu.SemaphoreType.DMA((2 + parts,))]
    act_shape, slope_shape = sd((seqs, bins, chans), BF16), sd((seqs, rows_e, chans), BF16)
    acts_scratch = pltpu.VMEM((seqs, rows_x, chans), BF16)
    taps = [kernels, taps_other]
    current = None
    saved = []
    for b in range(blocks - 1):
        scratch = [acts_scratch] + weight_scratch
        if b == 0:
            lead, specs = [inputs, lo, hi, inputs_other], [ANY] * 4
            scratch = scratch + [acts_scratch, pltpu.SemaphoreType.DMA((6 * seqs,))]
        else:
            lead, specs = [current], [VMEM]
        got = call(
            functools.partial(forward_kernel, b, b == 0, marks[b]),
            specs + [VMEM, VMEM, ANY, ANY, ANY],
            [sd((seqs, rows_x, chans), BF16)] + [act_shape, slope_shape] * (b + 1),
            scratch,
            8,
        )(*lead, *taps, mixers, near[b], far[b])
        current = got[0]
        saved += [tuple(got[1 + 2 * i : 3 + 2 * i]) for i in range(b + 1)]
        if b == 0:
            current, far[1], *third = join(current, far[1], *third)
            if share_bits > 2:
                third.append(flip(third[0], "seq", last_bits[2]))
        else:
            current, cot_other, *third = join(current, cot_other, *third)
            near[2] = jnp.concatenate([held[2], *third])
            far[2] = flip(near[2], "seq", 0)

    def both(own, received):
        many = seqs // len(received)

        def plan():
            return [(0, slice(None), 0, ours(0, everything))] + [
                (1 + i, slice(None), 0, theirs(i * many, everything, many)) for i in range(len(received))
            ]

        return pack(plan, 1 + len(received), [own, *received], [sd(inputs.shape, BF16)])[0]

    scale = 1.0 / math.sqrt(all_seqs * bins * n)
    count = n
    size = chans // n
    turned = pltpu.VMEM((count, size, seqs * bins), BF16 if size % 16 == 0 else F32)
    shares = [sd((2, count // 2, size, half), BF16)] * 2

    class Exchange:
        def __init__(self, keep, send, order):
            shape = (2,) * bits + (size, half)
            self.pieces = [keep.reshape(shape), flip(send, "seq", 0).reshape(shape)]
            self.dims = ["ch"] + list(range(bits - 1, 0, -1))
            self.order = list(order)

        def arrived(self, token):
            token, self.pieces[-1] = join(token, self.pieces[-1])
            return token

        def step(self):
            axis = self.order.pop(0)
            at = self.dims.index(axis)
            self.dims.pop(at)
            sent = sum(lax.index_in_dim(p, 1, at, keepdims=False).astype(F32) for p in self.pieces).astype(BF16)
            kept = [lax.index_in_dim(p, 0, at, keepdims=False) for p in self.pieces]
            self.pieces = kept + [flip(sent, "ch", 0) if axis == "ch" else flip(sent, "seq", axis)]
            return sent

        def result(self):
            return sum(p.astype(F32) for p in self.pieces)

    if bits == 4:
        orders = [["ch", 1, 2, 3], [1, 2, "ch", 3], [2, "ch", 1, 3]]
    else:
        orders = [list(range(1, bits)) + ["ch"]] * blocks

    top = blocks - 1
    act, slope = saved[top]
    upper, keep, send = call(
        functools.partial(turn_kernel, scale),
        [VMEM] + [ANY] * 4,
        [slope_shape] + shares,
        [turned, pltpu.SemaphoreType.DMA((6 * seqs,))],
        5,
    )(act, cotangent, lo, hi, cot_other)
    act, far[2], send = join(act, far[2], send)
    exchanges = [None] * blocks
    exchanges[top] = Exchange(keep, send, orders[top])
    for b in range(top, -1, -1):
        weights = [*taps, mixers, near[b], far[b]]
        slope = saved[b][1]
        scratch = weight_scratch
        if b == top:
            out_own, out_sent = call(
                functools.partial(output_kernel, b, marks[b]),
                [VMEM, VMEM, ANY, ANY, ANY],
                [seqs_shape] * 2,
                weight_scratch,
                4,
            )(current, act, mixers, near[b], far[b])
            out_received = [flip(out_sent, "ch", 0)]
            upper, out_own = join(upper, out_own)
            lead, outs = [upper, slope], [slope_shape]
        elif b:
            lead, outs = [upper, slope, saved[b][0]], [slope_shape] + shares
            scratch = scratch + [turned]
        else:
            lead, outs = [upper, slope], [seqs_shape] * 2
        got = call(
            functools.partial(backward_kernel, b, b == top, b == 0, marks[b], scale),
            [VMEM] * (len(lead) + 2) + [ANY, ANY, ANY],
            outs,
            scratch,
            8 if b == top else 6,
        )(*lead, *weights)
        if b == top:
            upper = got[0]
            upper, exchanges[b].pieces[-1] = join(upper, exchanges[b].pieces[-1])
        elif b:
            upper, keep, send = got
            exchanges[b] = Exchange(keep, send, orders[b])
        else:
            in_own, in_sent = got
        if b == 1:
            keep, send = call(
                functools.partial(gradient_kernel, scale),
                [VMEM] * 2,
                shares,
                [turned],
                4,
            )(saved[0][0], upper)
            send, out_received[0] = join(send, out_received[0])
            exchanges[0] = Exchange(keep, send, orders[0])
            for e in exchanges[:0:-1]:
                e.step()
            upper, exchanges[0].pieces[-1] = join(upper, exchanges[0].pieces[-1])
            exchanges[0].step()
    outputs = both(out_own, out_received)
    in_own, outputs, *arrived = join(in_own, outputs, *[e.pieces[-1] for e in exchanges])
    for e, piece in zip(exchanges, arrived):
        e.pieces[-1] = piece
        e.step()
    arrived = join(in_sent, *[e.pieces[-1] for e in exchanges])
    in_sent = arrived[0]
    for e, piece in zip(exchanges, arrived[1:]):
        e.pieces[-1] = piece
    token = fence(fetched[0, :16, :128], *[e.step() for e in exchanges], in_sent)
    in_received = flip(in_sent, "ch", 0)
    arrived = join(token, *[e.pieces[-1] for e in exchanges])
    token = arrived[0]
    for e, piece in zip(exchanges, arrived[1:]):
        e.pieces[-1] = piece
        while e.order:
            e.step()
    arrived = join(both(in_own, [in_received]), *[e.pieces[-1] for e in exchanges])
    input_grad = arrived[0]
    for e, piece in zip(exchanges, arrived[1:]):
        e.pieces[-1] = piece
    grads_token = token
    grads = [e.result() for e in exchanges]
    return outputs, input_grad, jnp.stack(grads)


def solution(mesh):
    placed = (P(None, "seq", "ch"), P(None, None, "ch"), P(None, None, "ch"), P(None, "seq", "ch"))
    return jax.shard_map(
        on_device,
        mesh=mesh,
        in_specs=placed,
        out_specs=(P(None, "seq", "ch"), P(None, "seq", "ch"), P(None, "seq", "ch")),
        check_vma=False,
    )
```
